32 devices in a mesh: ctx: 16 (over z, y, x), fsdp: 2 (over core).
Axes of the slice: x: 2, y: 2, z: 4, core: 2. Of those that a mesh axis runs over, the one named last changes fastest.
Arguments:
- tokens: bfloat16 [2, 2048, 4096], P('fsdp', 'ctx'), may hold values from -6 to 6
- queries: bfloat16 [2, 2048, 512], P('fsdp', 'ctx'), may hold values from -6 to 6
- flags: int32 [2, 2048], P('fsdp', 'ctx'), may hold values from 0 to 1, as said below
- w_key: bfloat16 [4096, 512], P(('ctx', 'fsdp')), may hold values from -0.09375 to 0.09375
- w_value: bfloat16 [4096, 512], P(('ctx', 'fsdp')), may hold values from -0.09375 to 0.09375
- norm_gain: float32 [512], replicated, may hold values from 0.25 to 1.75
Outputs:
- attended: bfloat16 [2, 2048, 512], P('fsdp', 'ctx')
The draws below stay inside these ranges and needn't reach their ends.
Inputs may be any that keep to these rules, and one draw needn't show every extreme that they name: `flags`: in each sequence a document starts at token 0 and at every token k * 1024 + 1024 // 2; other tokens start one at random, never before token 1536 and never at the first token of a block. No document is longer than 1024 tokens.
All inputs are finite; a program needn't handle non-finite values.
Results may differ from the reference program's by a relative error of at most 0.0053.
Values may be sent and summed in bfloat16 or wider, within the bound.
No kernel may reach another device: no remote copies, remote signals or barrier semaphores. Data moves between devices by JAX's collectives and lax.ppermute only.
A program may use at most 64 MiB of HBM per device.

```python
import jax
import jax.numpy as jnp
from jax import lax

D = 4096
HEAD = 128
HEADS = 4
TOK_DEV = 128
HD = 512
DOC_MOST = 1024
LEN = 2048
SEQS = 2
N_CTX = 16


def draw_flags(key, part):
    places = jnp.arange(LEN, dtype=jnp.int32)
    half_doc = DOC_MOST // 2
    forced = (places == 0) | (places % DOC_MOST == half_doc)
    picks = jax.random.randint(key, (SEQS, LEN), 0, 4 * TOK_DEV)
    allowed = (places >= DOC_MOST + half_doc) & (places % TOK_DEV != 0)
    extra = (picks == 0) & allowed[None, :]
    return (forced[None, :] | extra).astype(jnp.int32)


def shard_levels(rng, shape, pieces, least, largest):
    level, own = 1.0, jax.random.fold_in(rng, 6)
    for dim, blocks in pieces:
        steps = jnp.exp(jax.random.uniform(jax.random.fold_in(own, dim), (blocks,), jnp.float32, least / len(pieces), largest / len(pieces)))
        level = level * jnp.repeat(steps, shape[dim] // blocks).reshape([-1 if axis == dim else 1 for axis in range(len(shape))])
    return level


def gaussian(rng, dims, spread, bound, cuts=(), kind=jnp.bfloat16):
    values = jax.random.normal(rng, dims, jnp.float32) * spread
    if len(cuts) > 0:
        values = shard_levels(rng, dims, cuts, -0.22, 0.18) * values
    return jnp.clip(values, min=-bound, max=bound).astype(kind)


def setup_inputs(seed: int = 0) -> dict:
    keys = jax.random.split(jax.random.key(seed), 7)
    return {
        "tokens": gaussian(keys[0], (SEQS, LEN, D), 1.0, 6.0, ((0, 2), (1, 16))),
        "queries": gaussian(keys[1], (SEQS, LEN, HD), 1.0, 6.0, ((0, 2), (1, 16))),
        "flags": draw_flags(jax.random.fold_in(keys[6], 71), 0),
        "w_key": gaussian(keys[3], (D, HD), D ** -0.5, 0.09375, ((0, 32),)),
        "w_value": gaussian(keys[4], (D, HD), D ** -0.5, 0.09375, ((0, 32),)),
        "norm_gain": jnp.clip(1.0 + 0.15 * jax.random.normal(keys[5], (HD,), jnp.float32), 0.25, 1.75),
    }


def feature(u):
    return jax.nn.elu(u) + 1.0

def block_step(norm_gain, carried, item):
    query, key, value, marks = item
    seg = jnp.cumsum(marks).astype(jnp.int32)
    last = seg[TOK_DEV - 1]
    reset = (last > 0).astype(jnp.float32)
    tail = (seg == last).astype(key.dtype)
    local_state = jnp.einsum('the,thf->hef', (key * tail[:, None, None]).astype(jnp.float32), value.astype(jnp.float32))
    carried_b = carried.astype(jnp.bfloat16)
    first = (seg == 0).astype(jnp.float32)
    carried_term = jnp.einsum('the,hef->thf', query.astype(jnp.float32), carried_b.astype(jnp.float32)) * first[:, None, None]
    places = jnp.arange(TOK_DEV, dtype=jnp.int32)
    allowed = (places[None, :] <= places[:, None]) & (seg[None, :] == seg[:, None])
    scores = jnp.einsum('the,she->hts', query.astype(jnp.float32), key.astype(jnp.float32))
    scores = jnp.where(allowed[None, :, :], scores, 0.0).astype(jnp.bfloat16)
    inside = jnp.einsum('hts,shf->thf', scores.astype(jnp.float32), value.astype(jnp.float32))
    mixed = carried_term + inside
    scale = lax.rsqrt(lax.optimization_barrier(jnp.mean(mixed * mixed, axis=-1, keepdims=True)) + 1e-06)
    attended = (mixed * scale * norm_gain.reshape(HEADS, HEAD)).astype(jnp.bfloat16)
    new_carried = (1.0 - reset) * carried + local_state
    return (new_carried, attended)

def reference(tokens, queries, flags, w_key, w_value, norm_gain):
    results = []
    for seq in range(SEQS):
        key = feature(jnp.dot(tokens[seq], w_key, preferred_element_type=jnp.float32)).astype(jnp.bfloat16)
        value = jnp.dot(tokens[seq], w_value, preferred_element_type=jnp.float32).astype(jnp.bfloat16)
        query = feature(queries[seq].astype(jnp.float32)).astype(jnp.bfloat16)
        key = key.reshape(N_CTX, TOK_DEV, HEADS, HEAD)
        value = value.reshape(N_CTX, TOK_DEV, HEADS, HEAD)
        query = query.reshape(N_CTX, TOK_DEV, HEADS, HEAD)
        marks = flags[seq].reshape(N_CTX, TOK_DEV)
        start = jnp.zeros((HEADS, HEAD, HEAD), jnp.float32)
        final, blocks = lax.scan(lambda c, it: block_step(norm_gain, c, it), start, (query, key, value, marks))
        results.append(blocks.reshape(LEN, HD))
    return jnp.stack(results)
```

```python
import functools

import jax
import jax.numpy as jnp
from jax import lax
from jax.experimental import pallas as pl
from jax.experimental.pallas import tpu as pltpu
from jax.sharding import PartitionSpec as P

HEAD = 128
BF, F32 = jnp.bfloat16, jnp.float32
DOC_BLOCKS = {16: 8, 64: 16}


def phi(u):
    return jnp.where(u > 0, u + 1.0, jnp.exp(jnp.minimum(u, 0.0)))


def aligned(index, size):
    return pl.ds(pl.multiple_of(index * size, size), size)


def inner_outer(heads):
    me = lax.axis_index("ctx")
    return lax.rem(me, heads), lax.div(me, heads)


def pack_kernel(heads, tok_ref, query_ref, flag_ref, *out_refs):
    inner, _ = inner_outer(heads)
    count, depth = tok_ref.shape
    outer = depth // (heads * 2 * HEAD)
    marks = jnp.broadcast_to(flag_ref[...].astype(F32), (count, count)).astype(BF)
    for k, out in enumerate(out_refs):
        to = jnp.bitwise_xor(inner, k)
        for o in range(outer):
            out[:, o * 256 : (o + 1) * 256] = tok_ref[:, aligned(o * heads + to, 256)]
        cols = outer * 256
        out[:, cols : cols + HEAD] = phi(query_ref[:, aligned(to, HEAD)].astype(F32)).astype(BF)
        out[:, cols + HEAD :] = marks


def pack(tokens, queries, flags, heads, fsdp, rows):
    count, depth = tokens.shape
    share = fsdp * rows
    if share == 2 * HEAD:
        wide = depth // heads + 2 * HEAD
        return pl.pallas_call(
            functools.partial(pack_kernel, heads),
            out_shape=[jax.ShapeDtypeStruct((count, wide), BF)] * heads,
            name="pack",
        )(tokens, queries, flags)
    inner, _ = inner_outer(heads)
    by_inner = tokens.reshape(count, -1, heads, share).transpose(2, 0, 1, 3).reshape(heads, count, -1)
    query = phi(queries.astype(F32)).astype(BF).reshape(count, heads, HEAD).transpose(1, 0, 2)
    marks = jnp.broadcast_to(flags.astype(BF), (count, count))
    out = []
    for k in range(heads):
        to = jnp.bitwise_xor(inner, k)
        parts = [lax.dynamic_index_in_dim(a, to, 0, False) for a in (by_inner, query)]
        out.append(jnp.concatenate(parts + [marks], axis=1))
    return out


def product_kernel(heads, split, *refs):
    x_refs, w_refs = refs[:heads], refs[heads : -heads - 1]
    out_refs, tok = refs[-heads - 1 : -1], refs[-1]
    inner, outer = inner_outer(heads)
    count = x_refs[0].shape[0]
    for k, x in enumerate(x_refs):
        rows = aligned(jnp.bitwise_xor(inner, k), count)
        if split:
            core = lax.axis_index("fsdp")
            for i in range(len(w_refs)):
                at = jnp.bitwise_xor(outer, i // 2) * 2 + jnp.bitwise_xor(core, i % 2)
                tok[rows, i * HEAD : (i + 1) * HEAD] = x[:, aligned(at, HEAD)]
        else:
            tok[rows, :] = x[:, : tok.shape[1]]
    for k, out in list(enumerate(out_refs))[1:] + [(0, out_refs[0])]:
        cols = aligned(jnp.bitwise_xor(inner, k), 2 * HEAD)
        w = jnp.concatenate([w[:, cols] for w in w_refs], axis=0)
        out[...] = jnp.dot(tok[...], w, preferred_element_type=F32).astype(out.dtype)


def product(xs, ws, heads, split):
    count = xs[0].shape[0]
    depth = sum(w.shape[0] for w in ws)
    shape = (heads * count, 2 * HEAD)
    return pl.pallas_call(
        functools.partial(product_kernel, heads, split),
        out_shape=[jax.ShapeDtypeStruct(shape, F32)] + [jax.ShapeDtypeStruct(shape, BF)] * (heads - 1),
        scratch_shapes=[pltpu.VMEM((heads * count, depth), BF)],
        compiler_params=pltpu.CompilerParams(vmem_limit_bytes=40 * 2**20),
        name="product",
    )(*xs, *ws)


def inside_kernel(heads, *refs):
    parts, extras = refs[:heads], refs[heads : 2 * heads]
    state_ref, keep_ref, first_ref, inside_ref, query, marks = refs[2 * heads :]
    inner, _ = inner_outer(heads)
    count = extras[0].shape[0]
    total = heads * count
    for k, extra in enumerate(extras):
        at = jnp.bitwise_xor(inner, k)
        query[aligned(at, count), :] = extra[:, :HEAD]
        marks[:, aligned(at, count)] = extra[:, HEAD:]
    proj = parts[0][...]
    for part in parts[1:]:
        proj = proj + part[...].astype(F32)
    key = phi(proj[:, :HEAD]).astype(BF)
    value = proj[:, HEAD:].astype(BF)
    early = lax.broadcasted_iota(jnp.int32, (total, total), 0)
    late = lax.broadcasted_iota(jnp.int32, (total, total), 1)
    upto = jnp.where(early <= late, 1.0, 0.0).astype(BF)
    seg = jnp.dot(marks[...], upto, preferred_element_type=F32)
    seg_col = seg.T
    last = jnp.broadcast_to(seg_col[total - 1 :, :], (total, HEAD))
    tail = jnp.where(seg_col == last, value.astype(F32), 0.0).astype(BF)
    state_ref[...] = lax.dot_general(key, tail, (((0,), (0,)), ((), ())), preferred_element_type=F32)
    keep_ref[...] = jnp.where(last[:HEAD, :] == 0.0, 1.0, 0.0)
    first_ref[...] = jnp.where(seg_col == 0.0, query[...].astype(F32), 0.0).astype(BF)
    for i in range(heads):
        rows, width = slice(i * count, (i + 1) * count), (i + 1) * count
        scores = lax.dot_general(
            query[rows, :], key[:width, :], (((1,), (1,)), ((), ())), preferred_element_type=F32
        )
        own = jnp.concatenate([seg_col[rows, :]] * (i + 1), axis=1)
        allowed = (own == seg[:, :width]) & (late[:count, :width] <= early[rows, :width])
        scores = jnp.where(allowed, scores, 0.0).astype(BF)
        inside_ref[rows, :] = jnp.dot(scores, value[:width, :], preferred_element_type=F32)


def inside(parts, packed, heads):
    count, wide = packed[0].shape
    total = heads * count
    whole = pl.BlockSpec((total, 2 * HEAD), lambda i: (0, 0))
    extra = pl.BlockSpec((count, 2 * HEAD), lambda i: (0, wide // (2 * HEAD) - 1))
    square = jax.ShapeDtypeStruct((HEAD, HEAD), F32)
    return pl.pallas_call(
        functools.partial(inside_kernel, heads),
        grid=(1,),
        in_specs=[whole] * heads + [extra] * heads,
        out_shape=[
            square,
            square,
            jax.ShapeDtypeStruct((total, HEAD), BF),
            jax.ShapeDtypeStruct((total, HEAD), F32),
        ],
        out_specs=[
            pl.BlockSpec((HEAD, HEAD), lambda i: (0, 0)),
            pl.BlockSpec((HEAD, HEAD), lambda i: (0, 0)),
            pl.BlockSpec((total, HEAD), lambda i: (0, 0)),
            pl.BlockSpec((total, HEAD), lambda i: (0, 0)),
        ],
        scratch_shapes=[pltpu.VMEM((total, HEAD), BF), pltpu.VMEM((count, total), BF)],
        compiler_params=pltpu.CompilerParams(vmem_limit_bytes=40 * 2**20),
        name="inside",
    )(*parts, *packed)


def finish_kernel(heads, carried_ref, first_ref, inside_ref, gain_ref, *refs):
    out_refs, done = refs[:-1], refs[-1]
    inner, _ = inner_outer(heads)
    count = out_refs[0].shape[0]
    mixed = inside_ref[...] + jnp.dot(first_ref[...], carried_ref[...], preferred_element_type=F32)
    scale = lax.rsqrt(jnp.mean(mixed * mixed, axis=-1, keepdims=True) + 1e-06)
    done[...] = (mixed * scale * gain_ref[:, aligned(inner, HEAD)]).astype(BF)
    for k, out in enumerate(out_refs):
        out[...] = done[aligned(jnp.bitwise_xor(inner, k), count), :]


def finish(carried, first, within, gain, heads):
    total = first.shape[0]
    return pl.pallas_call(
        functools.partial(finish_kernel, heads),
        out_shape=[jax.ShapeDtypeStruct((total // heads, HEAD), BF)] * heads,
        scratch_shapes=[pltpu.VMEM((total, HEAD), BF)],
        name="finish",
    )(carried, first, within, gain)


def join_kernel(heads, *refs):
    inner, _ = inner_outer(heads)
    for k, part in enumerate(refs[:-1]):
        refs[-1][:, aligned(jnp.bitwise_xor(inner, k), HEAD)] = part[...]


def join(parts, heads):
    count = parts[0].shape[0]
    return pl.pallas_call(
        functools.partial(join_kernel, heads),
        out_shape=jax.ShapeDtypeStruct((count, heads * HEAD), BF),
        name="join",
    )(*parts)


def on_device(n_ctx, fsdp, tokens, queries, flags, w_key, w_value, norm_gain):
    rows, width = w_key.shape
    heads = width // HEAD
    outer = n_ctx // heads

    def swap(a, mask):
        return lax.ppermute(a, "ctx", [(i, i ^ mask) for i in range(n_ctx)])

    by_head = [w.reshape(rows, heads, HEAD) for w in (w_key, w_value)]
    weights = jnp.concatenate(by_head, axis=2).reshape(rows, 2 * width)
    packed = pack(tokens[0], queries[0], flags, heads, fsdp, rows)
    split = outer == 4 and fsdp == 2 and rows == HEAD
    if split:
        far = swap(weights, 3 * heads)
        near = swap(weights, heads)
        received = [packed[0]] + [swap(packed[k], k) for k in range(1, heads)]
        pieces = [weights, near, swap(far, heads), far]
        panels = []
        for piece in pieces:
            panels += [piece, lax.ppermute(piece, "fsdp", [(0, 1), (1, 0)])]
    else:
        received = [packed[0]] + [swap(packed[k], k) for k in range(1, heads)]
        groups = [[o * heads + q for o in range(outer)] for q in range(heads)]
        chip = lax.all_gather(weights, "fsdp", axis=0, tiled=True)
        panels = [lax.all_gather(chip, "ctx", axis=0, tiled=True, axis_index_groups=groups)]
    partial = product(received, panels, heads, split)
    parts = [partial[0]] + [swap(partial[k], k) for k in range(1, heads)]
    state, keep, first, within = inside(parts, received, heads)

    doc = DOC_BLOCKS.get(n_ctx, 2 * n_ctx)
    starts = [b for b in range(n_ctx) if b % doc == doc // 2]
    pairs = [
        (b, b + heads)
        for b in range(n_ctx - heads)
        if (b // heads + 1) * heads not in starts
    ]
    rounds = max(1, min(doc // heads, outer) - 1)
    carried = lax.ppermute(state.astype(BF), "ctx", pairs)
    for _ in range(rounds - 1):
        carried = lax.ppermute((state + keep * carried.astype(F32)).astype(BF), "ctx", pairs)
    done = finish(carried, first, within, norm_gain.reshape(1, width), heads)
    mine = [done[0]] + [swap(done[k], k) for k in range(1, heads)]
    return join(mine, heads)[None]


def solution(mesh):
    n_ctx, fsdp = mesh.shape["ctx"], mesh.shape["fsdp"]
    in_specs = (
        P("fsdp", "ctx", None),
        P("fsdp", "ctx", None),
        P("fsdp", "ctx"),
        P(("ctx", "fsdp"), None),
        P(("ctx", "fsdp"), None),
        P(),
    )
    return jax.shard_map(
        functools.partial(on_device, n_ctx, fsdp),
        mesh=mesh,
        in_specs=in_specs,
        out_specs=P("fsdp", "ctx", None),
        check_vma=False,
    )
```

```python
import functools

import jax
import jax.numpy as jnp
from jax import lax
from jax.experimental import pallas as pl
from jax.experimental.pallas import tpu as pltpu
from jax.sharding import PartitionSpec as P

HEAD = 128
BF, F32 = jnp.bfloat16, jnp.float32
DOC_BLOCKS = {16: 8, 64: 16}
MARKS = 16


def phi(u):
    return jnp.where(u > 0, u + 1.0, jnp.exp(jnp.minimum(u, 0.0)))


def aligned(index, size):
    return pl.ds(pl.multiple_of(index * size, size), size)


def inner_outer(heads):
    me = lax.axis_index("ctx")
    return lax.rem(me, heads), lax.div(me, heads)


def limit(mib):
    return pltpu.CompilerParams(vmem_limit_bytes=mib * 2**20)


def pack_kernel(heads, tok_ref, query_ref, flag_ref, key_ref, value_ref, *refs):
    weight_ref, out_refs = refs[0], refs[1 : 1 + heads]
    query, flag, extra, in_sems, tok_sems, out_sems = refs[1 + heads :]
    inner, _ = inner_outer(heads)
    count, depth = tok_ref.shape
    rows = key_ref.shape[0]
    squares = depth // (heads * HEAD)
    loads = [
        pltpu.make_async_copy(query_ref, query, in_sems.at[0]),
        pltpu.make_async_copy(flag_ref, flag, in_sems.at[1]),
    ]
    copies = [
        pltpu.make_async_copy(key_ref, weight_ref.at[:rows, :], in_sems.at[2]),
        pltpu.make_async_copy(value_ref, weight_ref.at[rows:, :], in_sems.at[3]),
    ]
    for k in list(range(1, heads)) + [0]:
        to = jnp.bitwise_xor(inner, k)
        for i in range(squares):
            at = ((i // 2) * heads + to) * 2 + i % 2
            copies.append(
                pltpu.make_async_copy(
                    tok_ref.at[:, aligned(at, HEAD)],
                    out_refs[k].at[i * count : (i + 1) * count, :],
                    tok_sems.at[k, i],
                )
            )
    for copy in loads + copies:
        copy.start()
    for copy in loads:
        copy.wait()
    marks = jnp.broadcast_to(flag[...].astype(F32), (MARKS, count)).astype(BF)
    for k, out in enumerate(out_refs):
        own = query[:, aligned(jnp.bitwise_xor(inner, k), HEAD)].astype(F32)
        extra[k, :count, :] = phi(own).astype(BF)
        extra[k, count:, :] = marks
        copy = pltpu.make_async_copy(extra.at[k], out.at[squares * count :, :], out_sems.at[k])
        copy.start()
        copies.append(copy)
    for copy in copies:
        copy.wait()


def pack(tokens, queries, flags, w_key, w_value, heads, fsdp):
    count, depth = tokens.shape
    rows, width = w_key.shape
    share, squares = fsdp * rows, depth // (heads * HEAD)
    if share == 2 * HEAD:
        shape = ((squares + 1) * count + MARKS, HEAD)
        hbm = pl.BlockSpec(memory_space=pl.ANY)
        weights, *packed = pl.pallas_call(
            functools.partial(pack_kernel, heads),
            in_specs=[hbm] * 5,
            out_specs=[hbm] * (1 + heads),
            out_shape=[jax.ShapeDtypeStruct((2 * rows, width), BF)]
            + [jax.ShapeDtypeStruct(shape, BF)] * heads,
            scratch_shapes=[
                pltpu.VMEM((count, width), BF),
                pltpu.VMEM((1, count), jnp.int32),
                pltpu.VMEM((heads, count + MARKS, HEAD), BF),
                pltpu.SemaphoreType.DMA((4,)),
                pltpu.SemaphoreType.DMA((heads, squares)),
                pltpu.SemaphoreType.DMA((heads,)),
            ],
            compiler_params=limit(60),
            name="pack",
        )(tokens, queries, flags, w_key, w_value)
        return weights, packed
    inner, _ = inner_outer(heads)
    by_inner = tokens.reshape(count, -1, heads, share).transpose(2, 0, 1, 3)
    by_inner = by_inner.reshape(heads, count, squares, HEAD).transpose(0, 2, 1, 3).reshape(heads, -1, HEAD)
    query = phi(queries.astype(F32)).astype(BF).reshape(count, heads, HEAD).transpose(1, 0, 2)
    marks = jnp.broadcast_to(flags.astype(BF), (MARKS, count))
    out = []
    for k in range(heads):
        to = jnp.bitwise_xor(inner, k)
        parts = [lax.dynamic_index_in_dim(a, to, 0, False) for a in (by_inner, query)]
        out.append(jnp.concatenate(parts + [marks], axis=0))
    return jnp.concatenate([w_key, w_value], axis=0), out


def product_kernel(heads, count, split, places, *refs):
    x_refs, w_refs = refs[:heads], refs[heads : -heads - 1]
    out_refs, tok = refs[-heads - 1 : -1], refs[-1]
    inner, outer = inner_outer(heads)
    squares = tok.shape[1] // HEAD
    half = tok.shape[1] // len(places)
    for k, x in enumerate(x_refs):
        rows = aligned(jnp.bitwise_xor(inner, k), count)
        for i in range(squares):
            at = i
            if split:
                core = lax.axis_index("fsdp")
                at = jnp.bitwise_xor(outer, i // 2) * 2 + jnp.bitwise_xor(core, i % 2)
            tok[rows, i * HEAD : (i + 1) * HEAD] = x[aligned(at, count), :]
    for k in list(range(1, heads)) + [0]:
        cols = aligned(jnp.bitwise_xor(inner, k), HEAD)
        key = jnp.concatenate([w_refs[j][at : at + half, cols] for j, at in places], axis=0)
        value = jnp.concatenate([w_refs[j][at + half : at + 2 * half, cols] for j, at in places], axis=0)
        w = jnp.concatenate([key, value], axis=1)
        out = out_refs[k]
        out[...] = jnp.dot(tok[...], w, preferred_element_type=F32).astype(out.dtype)


def product(xs, ws, heads, count, split, places):
    depth = sum(w.shape[0] for w in ws) // 2
    shape = (heads * count, 2 * HEAD)
    return pl.pallas_call(
        functools.partial(product_kernel, heads, count, split, places),
        out_shape=[jax.ShapeDtypeStruct(shape, F32)] + [jax.ShapeDtypeStruct(shape, BF)] * (heads - 1),
        scratch_shapes=[pltpu.VMEM((heads * count, depth), BF)],
        compiler_params=limit(24),
        name="product",
    )(*xs, *ws)


def inside_kernel(heads, *refs):
    parts, queries, flags = refs[:heads], refs[heads : 2 * heads], refs[2 * heads : 3 * heads]
    state_ref, keep_ref, first_ref = refs[3 * heads : 3 * heads + 3]
    within_refs = refs[3 * heads + 3 : -3]
    query, marks, within = refs[-3:]
    inner, _ = inner_outer(heads)
    count = queries[0].shape[0]
    total = heads * count
    for k in range(heads):
        at = jnp.bitwise_xor(inner, k)
        query[aligned(at, count), :] = queries[k][...]
        marks[:, aligned(at, count)] = flags[k][...]
    proj = parts[0][...]
    for part in parts[1:]:
        proj = proj + part[...].astype(F32)
    key = phi(proj[:, :HEAD]).astype(BF)
    value = proj[:, HEAD:].astype(BF)
    early = lax.broadcasted_iota(jnp.int32, (total, total), 0)
    late = lax.broadcasted_iota(jnp.int32, (total, total), 1)
    upto = jnp.where(early <= late, 1.0, 0.0).astype(BF)
    seg = jnp.dot(marks[...], upto, preferred_element_type=F32)[:1, :]
    seg = jnp.broadcast_to(seg, (HEAD, total))
    seg_col = seg.T
    last = jnp.broadcast_to(seg_col[total - 1 :, :], (total, HEAD))
    tail = jnp.where(seg_col == last, value.astype(F32), 0.0).astype(BF)
    state = lax.dot_general(key, tail, (((0,), (0,)), ((), ())), preferred_element_type=F32)
    state_ref[...] = state.astype(state_ref.dtype)
    keep_ref[...] = jnp.where(last[:HEAD, :] == 0.0, 1.0, 0.0)
    within[...] = jnp.where(seg_col == 0.0, 1.0, 0.0)
    first_ref[...] = within[aligned(inner, count), :].astype(BF)
    for i in range(heads):
        rows, width = slice(i * count, (i + 1) * count), (i + 1) * count
        scores = lax.dot_general(
            query[rows, :], key[:width, :], (((1,), (1,)), ((), ())), preferred_element_type=F32
        )
        own = jnp.concatenate([seg_col[rows, :]] * (i + 1), axis=1)
        allowed = (own == seg[:, :width]) & (late[:count, :width] <= early[rows, :width])
        scores = jnp.where(allowed, scores, 0.0).astype(BF)
        within[rows, :] = jnp.dot(scores, value[:width, :], preferred_element_type=F32)
    for k, out in enumerate(within_refs):
        out[...] = within[aligned(jnp.bitwise_xor(inner, k), count), :].astype(out.dtype)


def inside(parts, packed, heads, count, kind):
    total = heads * count
    squares = (packed[0].shape[0] - MARKS) // count - 1

    def at(rows, cols, place=0):
        return pl.BlockSpec((rows, cols), lambda i: (place, 0))

    def shape(rows, cols, dtype):
        return jax.ShapeDtypeStruct((rows, cols), dtype)

    return pl.pallas_call(
        functools.partial(inside_kernel, heads),
        grid=(1,),
        in_specs=[at(total, 2 * HEAD)] * heads
        + [at(count, HEAD, squares)] * heads
        + [at(MARKS, HEAD, (squares + 1) * count // MARKS)] * heads,
        out_shape=[shape(HEAD, HEAD, kind), shape(HEAD, HEAD, F32), shape(count, HEAD, BF)]
        + [shape(count, HEAD, F32)]
        + [shape(count, HEAD, BF)] * (heads - 1),
        out_specs=[at(HEAD, HEAD)] * 2 + [at(count, HEAD)] * (heads + 1),
        scratch_shapes=[
            pltpu.VMEM((total, HEAD), BF),
            pltpu.VMEM((MARKS, total), BF),
            pltpu.VMEM((total, HEAD), F32),
        ],
        compiler_params=limit(24),
        name="inside",
    )(*parts, *packed, *packed)


def finish_kernel(heads, *refs):
    carried, within, queries = refs[:heads], refs[heads : 2 * heads], refs[2 * heads : 3 * heads]
    first_ref, gain_ref, out_ref = refs[3 * heads :]
    inner, _ = inner_outer(heads)
    for k in range(heads):
        cols = aligned(jnp.bitwise_xor(inner, k), HEAD)
        query = queries[k][...] * first_ref[...]
        mixed = within[k][...].astype(F32) + jnp.dot(query, carried[k][...], preferred_element_type=F32)
        scale = lax.rsqrt(jnp.mean(mixed * mixed, axis=-1, keepdims=True) + 1e-06)
        out_ref[:, cols] = (mixed * scale * gain_ref[:, cols]).astype(BF)


def finish(carried, within, packed, first, gain, heads):
    count = first.shape[0]
    squares = (packed[0].shape[0] - MARKS) // count - 1

    def at(rows, cols, place=0):
        return pl.BlockSpec((rows, cols), lambda i: (place, 0))

    return pl.pallas_call(
        functools.partial(finish_kernel, heads),
        grid=(1,),
        in_specs=[at(HEAD, HEAD)] * heads
        + [at(count, HEAD)] * heads
        + [at(count, HEAD, squares)] * heads
        + [at(count, HEAD), at(1, heads * HEAD)],
        out_shape=jax.ShapeDtypeStruct((count, heads * HEAD), BF),
        out_specs=at(count, heads * HEAD),
        compiler_params=limit(8),
        name="finish",
    )(*carried, *within, *packed, first, gain)


def on_device(n_ctx, fsdp, tokens, queries, flags, w_key, w_value, norm_gain):
    count = tokens.shape[1]
    rows, width = w_key.shape
    heads = width // HEAD
    outer = n_ctx // heads

    def swap(a, mask):
        return lax.ppermute(a, "ctx", [(i, i ^ mask) for i in range(n_ctx)])

    split = outer == 4 and fsdp == 2 and rows == HEAD
    weights, packed = pack(tokens[0], queries[0], flags, w_key, w_value, heads, fsdp)
    if split:
        far = swap(weights, 3 * heads)
        near = swap(weights, heads)
    received = [packed[0]] + [swap(packed[k], k) for k in range(1, heads)]
    if split:
        far, near, *received = lax.optimization_barrier((far, near, *received))
        last = swap(far, heads)
        early = jnp.concatenate([weights, near, far], axis=0)
        early, last_other = [lax.ppermute(w, "fsdp", [(0, 1), (1, 0)]) for w in (early, last)]
        panels = [weights, near, last, far, early, last_other]
        places = [(0, 0), (4, 0), (1, 0), (4, 2 * rows), (2, 0), (5, 0), (3, 0), (4, 4 * rows)]
    else:
        groups = [[o * heads + q for o in range(outer)] for q in range(heads)]
        chip = [lax.all_gather(w, "fsdp", axis=0, tiled=True) for w in (w_key, w_value)]
        panels = [lax.all_gather(w, "ctx", axis=0, tiled=True, axis_index_groups=groups) for w in chip]
        panels, places = [jnp.concatenate(panels, axis=0)], [(0, 0)]
    partial = product(received, panels, heads, count, split, places)
    parts = [partial[0]] + [swap(partial[k], k) for k in range(1, heads)]

    doc = DOC_BLOCKS.get(n_ctx, 2 * n_ctx)
    starts = [b for b in range(n_ctx) if b % doc == doc // 2]
    pairs = [
        (b, b + heads)
        for b in range(n_ctx - heads)
        if (b // heads + 1) * heads not in starts
    ]
    rounds = max(1, min(doc // heads, outer) - 1)
    state, keep, first, *within = inside(parts, received, heads, count, BF if rounds == 1 else F32)
    leaving = state
    for _ in range(rounds - 1):
        carried = lax.ppermute(leaving.astype(BF), "ctx", pairs)
        leaving = state + keep * carried.astype(F32)
    leaving = leaving.astype(BF)
    carried = [lax.ppermute(leaving, "ctx", [(a, b ^ k) for a, b in pairs]) for k in range(heads)]
    within = [within[0]] + [swap(within[k], k) for k in range(1, heads)]
    return finish(carried, within, packed, first, norm_gain.reshape(1, width), heads)[None]


def solution(mesh):
    n_ctx, fsdp = mesh.shape["ctx"], mesh.shape["fsdp"]
    in_specs = (
        P("fsdp", "ctx", None),
        P("fsdp", "ctx", None),
        P("fsdp", "ctx"),
        P(("ctx", "fsdp"), None),
        P(("ctx", "fsdp"), None),
        P(),
    )
    return jax.shard_map(
        functools.partial(on_device, n_ctx, fsdp),
        mesh=mesh,
        in_specs=in_specs,
        out_specs=P("fsdp", "ctx", None),
        check_vma=False,
    )
```

```python
import functools

import jax
import jax.numpy as jnp
from jax import lax
from jax.experimental import pallas as pl
from jax.experimental.pallas import tpu as pltpu
from jax.sharding import PartitionSpec as P

HEAD = 128
BF, F32 = jnp.bfloat16, jnp.float32
DOC_BLOCKS = {16: 8, 64: 16}
MARKS = 16


def phi(u):
    return jnp.where(u > 0, u + 1.0, jnp.exp(jnp.minimum(u, 0.0)))


def aligned(index, size):
    return pl.ds(pl.multiple_of(index * size, size), size)


def inner_outer(heads):
    me = lax.axis_index("ctx")
    return lax.rem(me, heads), lax.div(me, heads)


def limit(mib):
    return pltpu.CompilerParams(vmem_limit_bytes=mib * 2**20)


def pack_kernel(heads, tok_ref, query_ref, flag_ref, *refs):
    out_refs, sems = refs[:heads], refs[heads]
    inner, _ = inner_outer(heads)
    count, depth = tok_ref.shape
    squares = depth // (heads * HEAD)
    copies = []
    for k in list(range(1, heads)) + [0]:
        to = jnp.bitwise_xor(inner, k)
        for i in range(squares):
            at = ((i // 2) * heads + to) * 2 + i % 2
            copy = pltpu.make_async_copy(
                tok_ref.at[:, aligned(at, HEAD)],
                out_refs[k].at[i * count : (i + 1) * count, :],
                sems.at[k, i],
            )
            copy.start()
            copies.append(copy)
    marks = jnp.broadcast_to(flag_ref[...].astype(F32), (MARKS, count)).astype(BF)
    for k, out in enumerate(out_refs):
        own = query_ref[:, aligned(jnp.bitwise_xor(inner, k), HEAD)].astype(F32)
        out[squares * count : (squares + 1) * count, :] = phi(own).astype(BF)
        out[(squares + 1) * count :, :] = marks
    for copy in copies:
        copy.wait()


def pack(tokens, queries, flags, heads, share):
    count, depth = tokens.shape
    squares = depth // (heads * HEAD)
    if share == 2 * HEAD:
        shape = ((squares + 1) * count + MARKS, HEAD)
        vmem = pl.BlockSpec(memory_space=pltpu.VMEM)
        return pl.pallas_call(
            functools.partial(pack_kernel, heads),
            in_specs=[pl.BlockSpec(memory_space=pl.ANY), vmem, vmem],
            out_specs=[vmem] * heads,
            out_shape=[jax.ShapeDtypeStruct(shape, BF)] * heads,
            scratch_shapes=[pltpu.SemaphoreType.DMA((heads, squares))],
            compiler_params=limit(60),
            name="pack",
        )(tokens, queries, flags)
    inner, _ = inner_outer(heads)
    by_inner = tokens.reshape(count, -1, heads, share).transpose(2, 0, 1, 3)
    by_inner = by_inner.reshape(heads, count, squares, HEAD).transpose(0, 2, 1, 3).reshape(heads, -1, HEAD)
    query = phi(queries.astype(F32)).astype(BF).reshape(count, heads, HEAD).transpose(1, 0, 2)
    marks = jnp.broadcast_to(flags.astype(BF), (MARKS, count))
    out = []
    for k in range(heads):
        to = jnp.bitwise_xor(inner, k)
        parts = [lax.dynamic_index_in_dim(a, to, 0, False) for a in (by_inner, query)]
        out.append(jnp.concatenate(parts + [marks], axis=0))
    return out


def shape(rows, cols, dtype):
    return jax.ShapeDtypeStruct((rows, cols), dtype)


def assemble_kernel(heads, count, split, *refs):
    x_refs = refs[:heads]
    tok, query, first, seg_row, seg_col, marks = refs[heads:]
    inner, outer = inner_outer(heads)
    squares = tok.shape[1] // HEAD
    total = heads * count
    for k, x in enumerate(x_refs):
        place = jnp.bitwise_xor(inner, k)
        rows = aligned(place, count)
        for i in range(squares):
            at = i
            if split:
                core = lax.axis_index("fsdp")
                at = jnp.bitwise_xor(outer, i // 2) * 2 + jnp.bitwise_xor(core, i % 2)
            tok[rows, i * HEAD : (i + 1) * HEAD] = x[aligned(at, count), :]
        query[rows, :] = x[squares * count : (squares + 1) * count, :]
        marks[:, rows] = x[(squares + 1) * count :, :]
    early = lax.broadcasted_iota(jnp.int32, (total, total), 0)
    late = lax.broadcasted_iota(jnp.int32, (total, total), 1)
    upto = jnp.where(early <= late, 1.0, 0.0).astype(BF)
    seg = jnp.dot(marks[...], upto, preferred_element_type=F32)[:1, :]
    seg_row[...] = jnp.broadcast_to(seg, seg_row.shape)
    col = jnp.broadcast_to(seg, (HEAD, total)).T
    seg_col[...] = col
    first[...] = jnp.where(col == 0.0, query[...].astype(F32), 0.0).astype(BF)


def assemble(received, heads, count, depth, split):
    total = heads * count
    return pl.pallas_call(
        functools.partial(assemble_kernel, heads, count, split),
        out_shape=[
            shape(total, depth, BF),
            shape(total, HEAD, BF),
            shape(total, HEAD, BF),
            shape(8, total, F32),
            shape(total, HEAD, F32),
        ],
        scratch_shapes=[pltpu.VMEM((MARKS, total), BF)],
        compiler_params=limit(16),
        cost_estimate=pl.CostEstimate(flops=4 * 10**9, bytes_accessed=0, transcendentals=0),
        name="assemble",
    )(*received)


def product_kernel(heads, places, tok, *refs):
    w_refs, out_refs = refs[:-heads], refs[-heads:]
    inner, _ = inner_outer(heads)
    half = tok.shape[1] // len(places)
    for k in list(range(1, heads)) + [0]:
        cols = aligned(jnp.bitwise_xor(inner, k), HEAD)
        key = jnp.concatenate([w_refs[j][at : at + half, cols] for j, at in places], axis=0)
        value = jnp.concatenate([w_refs[j][at + half : at + 2 * half, cols] for j, at in places], axis=0)
        w = jnp.concatenate([key, value], axis=1)
        out = out_refs[k]
        out[...] = jnp.dot(tok[...], w, preferred_element_type=F32).astype(out.dtype)


def product(tok, ws, heads, places):
    total = tok.shape[0]
    return pl.pallas_call(
        functools.partial(product_kernel, heads, places),
        out_shape=[shape(total, 2 * HEAD, F32)] + [shape(total, 2 * HEAD, BF)] * (heads - 1),
        compiler_params=limit(24),
        name="product",
    )(tok, *ws)


def state_kernel(heads, *refs):
    parts, seg_col = refs[:heads], refs[heads]
    state_ref, key_ref, value_ref = refs[heads + 1 :]
    proj = parts[0][...]
    for part in parts[1:]:
        proj = proj + part[...].astype(F32)
    key = phi(proj[:, :HEAD]).astype(BF)
    value = proj[:, HEAD:].astype(BF)
    last = seg_col[seg_col.shape[0] - 1 :, :]
    tail = jnp.where(seg_col[...] == last, value.astype(F32), 0.0).astype(BF)
    state = lax.dot_general(key, tail, (((0,), (0,)), ((), ())), preferred_element_type=F32)
    state_ref[...] = state.astype(state_ref.dtype)
    key_ref[...] = key
    value_ref[...] = value


def leave(parts, seg_col, heads, kind):
    total = seg_col.shape[0]
    return pl.pallas_call(
        functools.partial(state_kernel, heads),
        out_shape=[shape(HEAD, HEAD, kind), shape(total, HEAD, BF), shape(total, HEAD, BF)],
        compiler_params=limit(16),
        name="state",
    )(*parts, seg_col)


def within_kernel(heads, query, key, value, seg_row, seg_col, out_ref):
    total = query.shape[0]
    count = total // heads
    for i in range(heads):
        rows, width = slice(i * count, (i + 1) * count), (i + 1) * count
        scores = lax.dot_general(
            query[rows, :], key[:width, :], (((1,), (1,)), ((), ())), preferred_element_type=F32
        )
        own = jnp.concatenate([seg_col[rows, :]] * (i + 1), axis=1)
        early = lax.broadcasted_iota(jnp.int32, (count, width), 1)
        late = lax.broadcasted_iota(jnp.int32, (count, width), 0) + i * count
        allowed = (own == seg_row[:1, :width]) & (early <= late)
        scores = jnp.where(allowed, scores, 0.0).astype(BF)
        out_ref[rows, :] = jnp.dot(scores, value[:width, :], preferred_element_type=F32)


def within(query, key, value, seg_row, seg_col, heads):
    return pl.pallas_call(
        functools.partial(within_kernel, heads),
        out_shape=shape(query.shape[0], HEAD, F32),
        compiler_params=limit(16),
        cost_estimate=pl.CostEstimate(flops=2 * 10**9, bytes_accessed=0, transcendentals=0),
        name="within",
    )(query, key, value, seg_row, seg_col)


def finish_kernel(heads, carried, first, inside, gain, *refs):
    out_refs, done = refs[:-1], refs[-1]
    inner, _ = inner_outer(heads)
    count = out_refs[0].shape[0]
    mixed = inside[...] + jnp.dot(first[...], carried[...], preferred_element_type=F32)
    scale = lax.rsqrt(jnp.mean(mixed * mixed, axis=-1, keepdims=True) + 1e-06)
    done[...] = (mixed * scale * gain[:, aligned(inner, HEAD)]).astype(BF)
    for k, out in enumerate(out_refs):
        out[...] = done[aligned(jnp.bitwise_xor(inner, k), count), :]


def finish(carried, first, inside, gain, heads):
    total = first.shape[0]
    return pl.pallas_call(
        functools.partial(finish_kernel, heads),
        out_shape=[shape(total // heads, HEAD, BF)] * heads,
        scratch_shapes=[pltpu.VMEM((total, HEAD), BF)],
        compiler_params=limit(8),
        name="finish",
    )(carried, first, inside, gain)


def join_kernel(heads, *refs):
    inner, _ = inner_outer(heads)
    for k, part in enumerate(refs[:-1]):
        refs[-1][:, aligned(jnp.bitwise_xor(inner, k), HEAD)] = part[...]


def join(parts, heads):
    return pl.pallas_call(
        functools.partial(join_kernel, heads),
        out_shape=shape(parts[0].shape[0], heads * HEAD, BF),
        compiler_params=limit(8),
        name="join",
    )(*parts)


def on_device(n_ctx, fsdp, tokens, queries, flags, w_key, w_value, norm_gain):
    _, count, depth = tokens.shape
    rows, width = w_key.shape
    heads = width // HEAD
    outer = n_ctx // heads

    def swap(a, mask):
        return lax.ppermute(a, "ctx", [(i, i ^ mask) for i in range(n_ctx)])

    split = outer == 4 and fsdp == 2 and rows == HEAD
    if split:
        weights = jnp.concatenate([w_key, w_value], axis=0)
        far = swap(weights, 3 * heads)
        near = swap(weights, heads)
    packed = pack(tokens[0], queries[0], flags, heads, fsdp * rows)
    received = [packed[0]] + [swap(packed[k], k) for k in range(1, heads)]
    tok, query, first, seg_row, seg_col = assemble(received, heads, count, depth // heads, split)
    if split:
        panels = []
        for piece in [weights, near, swap(far, heads), far]:
            panels += [piece, lax.ppermute(piece, "fsdp", [(0, 1), (1, 0)])]
    else:
        groups = [[o * heads + q for o in range(outer)] for q in range(heads)]
        chip = [lax.all_gather(w, "fsdp", axis=0, tiled=True) for w in (w_key, w_value)]
        panels = [lax.all_gather(w, "ctx", axis=0, tiled=True, axis_index_groups=groups) for w in chip]
        panels = [jnp.concatenate(panels, axis=0)]
    partial = product(tok, panels, heads, [(j, 0) for j in range(len(panels))])
    parts = [partial[0]] + [swap(partial[k], k) for k in range(1, heads)]

    doc = DOC_BLOCKS.get(n_ctx, 2 * n_ctx)
    starts = [b for b in range(n_ctx) if b % doc == doc // 2]
    pairs = [
        (b, b + heads)
        for b in range(n_ctx - heads)
        if (b // heads + 1) * heads not in starts
    ]
    rounds = max(1, min(doc // heads, outer) - 1)
    state, key, value = leave(parts, seg_col, heads, BF if rounds == 1 else F32)
    carried = lax.ppermute(state.astype(BF), "ctx", pairs)
    keep = (seg_col[-1:, :] == 0.0).astype(F32)
    for _ in range(rounds - 1):
        carried = lax.ppermute((state + keep * carried.astype(F32)).astype(BF), "ctx", pairs)
    inside = within(query, key, value, seg_row, seg_col, heads)
    done = finish(carried, first, inside, norm_gain.reshape(1, width), heads)
    return join([done[0]] + [swap(done[k], k) for k in range(1, heads)], heads)[None]


def solution(mesh):
    n_ctx, fsdp = mesh.shape["ctx"], mesh.shape["fsdp"]
    in_specs = (
        P("fsdp", "ctx", None),
        P("fsdp", "ctx", None),
        P("fsdp", "ctx"),
        P(("ctx", "fsdp"), None),
        P(("ctx", "fsdp"), None),
        P(),
    )
    return jax.shard_map(
        functools.partial(on_device, n_ctx, fsdp),
        mesh=mesh,
        in_specs=in_specs,
        out_specs=P("fsdp", "ctx", None),
        check_vma=False,
    )
```

```python
import functools

import jax
import jax.numpy as jnp
from jax import lax
from jax.experimental import pallas as pl
from jax.experimental.pallas import tpu as pltpu
from jax.sharding import PartitionSpec as P

HEAD = 128
BF, F32 = jnp.bfloat16, jnp.float32
DOC_BLOCKS = {16: 8, 64: 16}
MARKS = 16
PARTS = 4


def phi(u):
    return jnp.where(u > 0, u + 1.0, jnp.exp(jnp.minimum(u, 0.0)))


def aligned(index, size):
    return pl.ds(pl.multiple_of(index * size, size), size)


def inner_outer(heads):
    me = lax.axis_index("ctx")
    return lax.rem(me, heads), lax.div(me, heads)


def shape(rows, cols, dtype):
    return jax.ShapeDtypeStruct((rows, cols), dtype)


def limit(mib):
    return pltpu.CompilerParams(vmem_limit_bytes=mib * 2**20)


def stack_kernel(*refs):
    parts, out, sems = refs[:-2], refs[-2], refs[-1]
    copies, at = [], 0
    for i, part in enumerate(parts):
        rows = part.shape[0]
        copies.append(pltpu.make_async_copy(part, out.at[at : at + rows, :], sems.at[i]))
        copies[-1].start()
        at += rows
    for copy in copies:
        copy.wait()


def stack(*parts):
    rows = sum(a.shape[0] for a in parts)
    return pl.pallas_call(
        stack_kernel,
        in_specs=[pl.BlockSpec(memory_space=pl.ANY)] * len(parts),
        out_specs=pl.BlockSpec(memory_space=pltpu.VMEM),
        out_shape=pltpu.VMEM((rows, parts[0].shape[1]), BF),
        scratch_shapes=[pltpu.SemaphoreType.DMA((len(parts),))],
        compiler_params=limit(8),
        name="stack",
    )(*[pltpu.with_memory_space_constraint(a, pltpu.HBM) for a in parts])


def partners(heads):
    return [0] + list(range(heads - 1, 0, -1))


def pack_kernel(heads, tok_ref, query_ref, flag_ref, *refs):
    out_refs = refs[:heads]
    tok, query, flag, sems = refs[heads:]
    inner, _ = inner_outer(heads)
    count, depth = tok_ref.shape
    squares = depth // (heads * HEAD)
    part = count // PARTS
    pairs = [(query_ref, query), (flag_ref, flag)]
    for p in range(PARTS):
        rows = slice(p * part, (p + 1) * part)
        pairs.append((tok_ref.at[rows, :], tok.at[rows, :]))
    copies = [pltpu.make_async_copy(a, b, sems.at[i]) for i, (a, b) in enumerate(pairs)]
    for copy in copies:
        copy.start()
    for copy in copies[:2]:
        copy.wait()
    marks = jnp.broadcast_to(flag[...].astype(F32), (MARKS, count)).astype(BF)
    for k, out in enumerate(out_refs):
        own = query[:, aligned(jnp.bitwise_xor(inner, k), HEAD)].astype(F32)
        out[squares * count : (squares + 1) * count, :] = phi(own).astype(BF)
        out[(squares + 1) * count :, :] = marks
    for p, copy in enumerate(copies[2:]):
        copy.wait()
        for k, out in enumerate(out_refs):
            to = jnp.bitwise_xor(inner, k)
            for i in range(squares):
                at = ((i // 2) * heads + to) * 2 + i % 2
                rows = slice(i * count + p * part, i * count + (p + 1) * part)
                out[rows, :] = tok[p * part : (p + 1) * part, aligned(at, HEAD)]


def pack(tokens, queries, flags, heads, share):
    count, depth = tokens.shape
    squares = depth // (heads * HEAD)
    if share == 2 * HEAD:
        packed = shape((squares + 1) * count + MARKS, HEAD, BF)
        return pl.pallas_call(
            functools.partial(pack_kernel, heads),
            in_specs=[pl.BlockSpec(memory_space=pl.ANY)] * 3,
            out_specs=[pl.BlockSpec(memory_space=pltpu.VMEM)] * heads,
            out_shape=[pltpu.VMEM(packed.shape, BF)] * heads,
            scratch_shapes=[
                pltpu.VMEM((count, depth), BF),
                pltpu.VMEM((count, heads * HEAD), BF),
                pltpu.VMEM((1, count), jnp.int32),
                pltpu.SemaphoreType.DMA((PARTS + 2,)),
            ],
            compiler_params=limit(8),
            name="pack",
        )(*[pltpu.with_memory_space_constraint(a, pltpu.HBM) for a in (tokens, queries, flags)])
    inner, _ = inner_outer(heads)
    by_inner = tokens.reshape(count, -1, heads, share).transpose(2, 0, 1, 3)
    by_inner = by_inner.reshape(heads, count, squares, HEAD).transpose(0, 2, 1, 3).reshape(heads, -1, HEAD)
    query = phi(queries.astype(F32)).astype(BF).reshape(count, heads, HEAD).transpose(1, 0, 2)
    marks = jnp.broadcast_to(flags.astype(BF), (MARKS, count))
    out = []
    for k in range(heads):
        to = jnp.bitwise_xor(inner, k)
        parts = [lax.dynamic_index_in_dim(a, to, 0, False) for a in (by_inner, query)]
        out.append(jnp.concatenate(parts + [marks], axis=0))
    return out


def assemble_kernel(heads, count, split, *refs):
    x_refs = refs[:heads]
    tok, query, first, seg_row, seg_col, marks = refs[heads:]
    inner, outer = inner_outer(heads)
    squares = tok.shape[1] // HEAD
    total = heads * count
    for k, x in zip(partners(heads), x_refs):
        place = jnp.bitwise_xor(inner, k)
        rows = aligned(place, count)
        for i in range(squares):
            at = i
            if split:
                core = lax.axis_index("fsdp")
                at = jnp.bitwise_xor(outer, i // 2) * 2 + jnp.bitwise_xor(core, i % 2)
            tok[rows, i * HEAD : (i + 1) * HEAD] = x[aligned(at, count), :]
        query[rows, :] = x[squares * count : (squares + 1) * count, :]
        marks[:, rows] = x[(squares + 1) * count :, :]
    early = lax.broadcasted_iota(jnp.int32, (total, total), 0)
    late = lax.broadcasted_iota(jnp.int32, (total, total), 1)
    upto = jnp.where(early <= late, 1.0, 0.0).astype(BF)
    seg = jnp.dot(marks[...], upto, preferred_element_type=F32)[:1, :]
    seg_row[...] = jnp.broadcast_to(seg, seg_row.shape)
    col = jnp.broadcast_to(seg, (HEAD, total)).T
    seg_col[...] = col
    first[...] = jnp.where(col == 0.0, query[...].astype(F32), 0.0).astype(BF)


def assemble(received, heads, count, depth, split):
    total = heads * count
    return pl.pallas_call(
        functools.partial(assemble_kernel, heads, count, split),
        out_shape=[
            shape(total, depth, BF),
            shape(total, HEAD, BF),
            shape(total, HEAD, BF),
            shape(8, total, F32),
            shape(total, HEAD, F32),
        ],
        scratch_shapes=[pltpu.VMEM((MARKS, total), BF)],
        compiler_params=limit(16),
        cost_estimate=pl.CostEstimate(flops=4 * 10**9, bytes_accessed=0, transcendentals=0),
        name="assemble",
    )(*received)


def product_kernel(heads, places, tok, *refs):
    w_refs, out_refs = refs[:-heads], refs[-heads:]
    inner, _ = inner_outer(heads)
    rows = tok.shape[1] // len(places)

    def panel(k):
        cols = aligned(jnp.bitwise_xor(inner, k), HEAD)
        return jnp.concatenate([w[at : at + rows, cols] for w, at in zip(w_refs, places)], axis=0)

    order = list(range(1, heads)) + [0]
    for a, b in zip(order[::2], order[1::2]):
        both = jnp.concatenate([panel(a), panel(b)], axis=1)
        both = jnp.dot(tok[...], both, preferred_element_type=F32)
        out_refs[a][...] = both[:, :HEAD].astype(out_refs[a].dtype)
        out_refs[b][...] = both[:, HEAD:].astype(out_refs[b].dtype)


def product(tok, ws, heads, name):
    total = tok.shape[0]
    return pl.pallas_call(
        functools.partial(product_kernel, heads, [at for _, at in ws]),
        out_shape=[shape(total, HEAD, F32)] + [shape(total, HEAD, BF)] * (heads - 1),
        compiler_params=limit(16),
        name=name,
    )(tok, *[w for w, _ in ws])


def gathered(parts):
    proj = parts[0][...]
    for part in parts[1:]:
        proj = proj + part[...].astype(F32)
    return proj


def score_kernel(heads, *refs):
    parts = refs[:heads]
    query, seg_row, seg_col, key_ref, score_ref = refs[heads:]
    total = query.shape[0]
    count = total // heads
    key = phi(gathered(parts)).astype(BF)
    key_ref[...] = key
    for i in range(heads):
        rows, width = slice(i * count, (i + 1) * count), (i + 1) * count
        scores = lax.dot_general(
            query[rows, :], key[:width, :], (((1,), (1,)), ((), ())), preferred_element_type=F32
        )
        own = jnp.concatenate([seg_col[rows, :]] * (i + 1), axis=1)
        early = lax.broadcasted_iota(jnp.int32, (count, width), 1)
        late = lax.broadcasted_iota(jnp.int32, (count, width), 0) + i * count
        allowed = (own == seg_row[:1, :width]) & (early <= late)
        score_ref[rows, :width] = jnp.where(allowed, scores, 0.0).astype(BF)


def score(parts, query, seg_row, seg_col, heads):
    total = query.shape[0]
    return pl.pallas_call(
        functools.partial(score_kernel, heads),
        out_shape=[shape(total, HEAD, BF), shape(total, total, BF)],
        compiler_params=limit(16),
        cost_estimate=pl.CostEstimate(flops=4 * 10**9, bytes_accessed=0, transcendentals=0),
        name="score",
    )(*parts, query, seg_row, seg_col)


def state_kernel(heads, *refs):
    parts = refs[:heads]
    key, seg_col, state_ref, value_ref = refs[heads:]
    value = gathered(parts).astype(BF)
    last = seg_col[seg_col.shape[0] - 1 :, :]
    tail = jnp.where(seg_col[...] == last, value.astype(F32), 0.0).astype(BF)
    state = lax.dot_general(key[...], tail, (((0,), (0,)), ((), ())), preferred_element_type=F32)
    state_ref[...] = state.astype(state_ref.dtype)
    value_ref[...] = value


def leave(parts, key, seg_col, heads, kind):
    total = seg_col.shape[0]
    return pl.pallas_call(
        functools.partial(state_kernel, heads),
        out_shape=[shape(HEAD, HEAD, kind), shape(total, HEAD, BF)],
        compiler_params=limit(16),
        name="state",
    )(*parts, key, seg_col)


def within_kernel(heads, scores, value, out_ref):
    count = value.shape[0] // heads
    for i in range(heads):
        rows, width = slice(i * count, (i + 1) * count), (i + 1) * count
        out_ref[rows, :] = jnp.dot(scores[rows, :width], value[:width, :], preferred_element_type=F32)


def within(scores, value, heads):
    return pl.pallas_call(
        functools.partial(within_kernel, heads),
        out_shape=shape(value.shape[0], HEAD, F32),
        compiler_params=limit(16),
        cost_estimate=pl.CostEstimate(flops=2 * 10**9, bytes_accessed=0, transcendentals=0),
        name="within",
    )(scores, value)


def finish_kernel(heads, carried, first, inside, gain, *refs):
    out_refs, done = refs[:-1], refs[-1]
    inner, _ = inner_outer(heads)
    count = out_refs[0].shape[0]
    mixed = inside[...] + jnp.dot(first[...], carried[...], preferred_element_type=F32)
    scale = lax.rsqrt(jnp.mean(mixed * mixed, axis=-1, keepdims=True) + 1e-06)
    done[...] = (mixed * scale * gain[:, aligned(inner, HEAD)]).astype(BF)
    for k, out in enumerate(out_refs):
        out[...] = done[aligned(jnp.bitwise_xor(inner, k), count), :]


def finish(carried, first, inside, gain, heads):
    total = first.shape[0]
    return pl.pallas_call(
        functools.partial(finish_kernel, heads),
        out_shape=[shape(total // heads, HEAD, BF)] * heads,
        scratch_shapes=[pltpu.VMEM((total, HEAD), BF)],
        compiler_params=limit(8),
        name="finish",
    )(carried, first, inside, gain)


def join_kernel(heads, *refs):
    inner, _ = inner_outer(heads)
    for k, part in zip(partners(heads), refs[:-1]):
        refs[-1][:, aligned(jnp.bitwise_xor(inner, k), HEAD)] = part[...]


def join(parts, heads):
    return pl.pallas_call(
        functools.partial(join_kernel, heads),
        out_shape=shape(parts[0].shape[0], heads * HEAD, BF),
        compiler_params=limit(8),
        name="join",
    )(*parts)


def on_device(n_ctx, fsdp, tokens, queries, flags, w_key, w_value, norm_gain):
    _, count, depth = tokens.shape
    rows, width = w_key.shape
    heads = width // HEAD
    outer = n_ctx // heads

    def swap(a, mask):
        return lax.ppermute(a, "ctx", [(i, i ^ mask) for i in range(n_ctx)])

    def exchange(parts):
        return [parts[0]] + [swap(parts[k], k) for k in partners(heads)[1:]]

    def other(a):
        return lax.ppermute(a, "fsdp", [(0, 1), (1, 0)])

    both = (w_key, w_value)
    split = outer == 4 and fsdp == 2 and rows == HEAD
    if split:
        weights = stack(*both)
        far = swap(weights, 3 * heads)
        near = swap(weights, heads)
    packed = pack(tokens[0], queries[0], flags, heads, fsdp * rows)
    received = exchange(packed)
    tok, query, first, seg_row, seg_col = assemble(received, heads, count, depth // heads, split)
    if split:
        whole = [(w, other(w)) for w in (weights, near, far)]
        panels = []
        for at in (0, rows):
            last = swap(far[at : at + rows], heads)
            own, close, away = [[(w, at) for w in pair] for pair in whole]
            panels.append(own + close + [(last, 0), (other(last), 0)] + away)
    else:
        groups = [[o * heads + q for o in range(outer)] for q in range(heads)]
        chip = [lax.all_gather(w, "fsdp", axis=0, tiled=True) for w in both]
        panels = [
            [(lax.all_gather(w, "ctx", axis=0, tiled=True, axis_index_groups=groups), 0)] for w in chip
        ]
    parts = []
    for panel, name in zip(panels, ("key_product", "value_product")):
        partial = product(tok, panel, heads, name)
        parts.append(exchange(partial))
    key, scores = score(parts[0], query, seg_row, seg_col, heads)

    doc = DOC_BLOCKS.get(n_ctx, 2 * n_ctx)
    starts = [b for b in range(n_ctx) if b % doc == doc // 2]
    pairs = [
        (b, b + heads)
        for b in range(n_ctx - heads)
        if (b // heads + 1) * heads not in starts
    ]
    rounds = max(1, min(doc // heads, outer) - 1)
    state, value = leave(parts[1], key, seg_col, heads, BF if rounds == 1 else F32)
    carried = lax.ppermute(state.astype(BF), "ctx", pairs)
    keep = (seg_col[-1:, :] == 0.0).astype(F32)
    for _ in range(rounds - 1):
        carried = lax.ppermute((state + keep * carried.astype(F32)).astype(BF), "ctx", pairs)
    inside = within(scores, value, heads)
    done = finish(carried, first, inside, norm_gain.reshape(1, width), heads)
    return join(exchange(done), heads)[None]


def solution(mesh):
    n_ctx, fsdp = mesh.shape["ctx"], mesh.shape["fsdp"]
    in_specs = (
        P("fsdp", "ctx", None),
        P("fsdp", "ctx", None),
        P("fsdp", "ctx"),
        P(("ctx", "fsdp"), None),
        P(("ctx", "fsdp"), None),
        P(),
    )
    return jax.shard_map(
        functools.partial(on_device, n_ctx, fsdp),
        mesh=mesh,
        in_specs=in_specs,
        out_specs=P("fsdp", "ctx", None),
        check_vma=False,
    )
```

```python
import functools

import jax
import jax.numpy as jnp
from jax import lax
from jax.experimental import pallas as pl
from jax.experimental.pallas import tpu as pltpu
from jax.sharding import PartitionSpec as P

HEAD = 128
BF, F32 = jnp.bfloat16, jnp.float32
DOC_BLOCKS = {16: 8, 64: 16}
MARKS = 16
PARTS = 4


def phi(u):
    return jnp.where(u > 0, u + 1.0, jnp.exp(jnp.minimum(u, 0.0)))


def aligned(index, size):
    return pl.ds(pl.multiple_of(index * size, size), size)


def inner_outer(heads):
    me = lax.axis_index("ctx")
    return lax.rem(me, heads), lax.div(me, heads)


def shape(rows, cols, dtype):
    return jax.ShapeDtypeStruct((rows, cols), dtype)


def limit(mib):
    return pltpu.CompilerParams(vmem_limit_bytes=mib * 2**20)


def stack_kernel(*refs):
    parts, out, sems = refs[:-2], refs[-2], refs[-1]
    copies, at = [], 0
    for i, part in enumerate(parts):
        rows = part.shape[0]
        copies.append(pltpu.make_async_copy(part, out.at[at : at + rows, :], sems.at[i]))
        copies[-1].start()
        at += rows
    for copy in copies:
        copy.wait()


def stack(*parts):
    rows = sum(a.shape[0] for a in parts)
    return pl.pallas_call(
        stack_kernel,
        in_specs=[pl.BlockSpec(memory_space=pl.ANY)] * len(parts),
        out_specs=pl.BlockSpec(memory_space=pltpu.VMEM),
        out_shape=pltpu.VMEM((rows, parts[0].shape[1]), BF),
        scratch_shapes=[pltpu.SemaphoreType.DMA((len(parts),))],
        compiler_params=limit(8),
        name="stack",
    )(*[pltpu.with_memory_space_constraint(a, pltpu.HBM) for a in parts])


def partners(heads):
    return [0] + list(range(heads - 1, 0, -1))


def pack_kernel(heads, tok_ref, query_ref, flag_ref, *refs):
    out_refs = refs[:heads]
    tok, query, flag, sems = refs[heads:]
    inner, _ = inner_outer(heads)
    count, depth = tok_ref.shape
    squares = depth // (heads * HEAD)
    part = count // PARTS
    pairs = [(query_ref, query), (flag_ref, flag)]
    for p in range(PARTS):
        rows = slice(p * part, (p + 1) * part)
        pairs.append((tok_ref.at[rows, :], tok.at[rows, :]))
    copies = [pltpu.make_async_copy(a, b, sems.at[i]) for i, (a, b) in enumerate(pairs)]
    for copy in copies:
        copy.start()
    for copy in copies[:2]:
        copy.wait()
    marks = jnp.broadcast_to(flag[...].astype(F32), (MARKS, count)).astype(BF)
    for k, out in enumerate(out_refs):
        own = query[:, aligned(jnp.bitwise_xor(inner, k), HEAD)].astype(F32)
        out[squares * count : (squares + 1) * count, :] = phi(own).astype(BF)
        out[(squares + 1) * count :, :] = marks
    for p, copy in enumerate(copies[2:]):
        copy.wait()
        for k, out in enumerate(out_refs):
            to = jnp.bitwise_xor(inner, k)
            for i in range(squares):
                at = ((i // 2) * heads + to) * 2 + i % 2
                rows = slice(i * count + p * part, i * count + (p + 1) * part)
                out[rows, :] = tok[p * part : (p + 1) * part, aligned(at, HEAD)]


def pack(tokens, queries, flags, heads, share):
    count, depth = tokens.shape
    squares = depth // (heads * HEAD)
    if share == 2 * HEAD:
        packed = shape((squares + 1) * count + MARKS, HEAD, BF)
        return pl.pallas_call(
            functools.partial(pack_kernel, heads),
            in_specs=[pl.BlockSpec(memory_space=pl.ANY)] * 3,
            out_specs=[pl.BlockSpec(memory_space=pltpu.VMEM)] * heads,
            out_shape=[pltpu.VMEM(packed.shape, BF)] * heads,
            scratch_shapes=[
                pltpu.VMEM((count, depth), BF),
                pltpu.VMEM((count, heads * HEAD), BF),
                pltpu.VMEM((1, count), jnp.int32),
                pltpu.SemaphoreType.DMA((PARTS + 2,)),
            ],
            compiler_params=limit(8),
            name="pack",
        )(*[pltpu.with_memory_space_constraint(a, pltpu.HBM) for a in (tokens, queries, flags)])
    inner, _ = inner_outer(heads)
    by_inner = tokens.reshape(count, -1, heads, share).transpose(2, 0, 1, 3)
    by_inner = by_inner.reshape(heads, count, squares, HEAD).transpose(0, 2, 1, 3).reshape(heads, -1, HEAD)
    query = phi(queries.astype(F32)).astype(BF).reshape(count, heads, HEAD).transpose(1, 0, 2)
    marks = jnp.broadcast_to(flags.astype(BF), (MARKS, count))
    out = []
    for k in range(heads):
        to = jnp.bitwise_xor(inner, k)
        parts = [lax.dynamic_index_in_dim(a, to, 0, False) for a in (by_inner, query)]
        out.append(jnp.concatenate(parts + [marks], axis=0))
    return out


def assemble_kernel(heads, count, split, *refs):
    x_refs = refs[:heads]
    tok, query, first, seg_row, seg_col, marks = refs[heads:]
    inner, outer = inner_outer(heads)
    squares = tok.shape[1] // HEAD
    total = heads * count
    for k, x in zip(partners(heads), x_refs):
        place = jnp.bitwise_xor(inner, k)
        rows = aligned(place, count)
        for i in range(squares):
            at = i
            if split:
                core = lax.axis_index("fsdp")
                at = jnp.bitwise_xor(outer, i // 2) * 2 + jnp.bitwise_xor(core, i % 2)
            tok[rows, i * HEAD : (i + 1) * HEAD] = x[aligned(at, count), :]
        query[rows, :] = x[squares * count : (squares + 1) * count, :]
        marks[:, rows] = x[(squares + 1) * count :, :]
    early = lax.broadcasted_iota(jnp.int32, (total, total), 0)
    late = lax.broadcasted_iota(jnp.int32, (total, total), 1)
    upto = jnp.where(early <= late, 1.0, 0.0).astype(BF)
    seg = jnp.dot(marks[...], upto, preferred_element_type=F32)[:1, :]
    seg_row[...] = jnp.broadcast_to(seg, seg_row.shape)
    col = jnp.broadcast_to(seg, (HEAD, total)).T
    seg_col[...] = col
    first[...] = jnp.where(col == 0.0, query[...].astype(F32), 0.0).astype(BF)


def assemble(received, heads, count, depth, split):
    total = heads * count
    return pl.pallas_call(
        functools.partial(assemble_kernel, heads, count, split),
        out_shape=[
            shape(total, depth, BF),
            shape(total, HEAD, BF),
            shape(total, HEAD, BF),
            shape(8, total, F32),
            shape(total, HEAD, F32),
        ],
        scratch_shapes=[pltpu.VMEM((MARKS, total), BF)],
        compiler_params=limit(16),
        cost_estimate=pl.CostEstimate(flops=4 * 10**9, bytes_accessed=0, transcendentals=0),
        name="assemble",
    )(*received)


def product_kernel(heads, places, tok, *refs):
    w_refs, out_refs = refs[:-heads], refs[-heads:]
    inner, _ = inner_outer(heads)
    rows = tok.shape[1] // len(places)

    def panel(k):
        cols = aligned(jnp.bitwise_xor(inner, k), HEAD)
        return jnp.concatenate([w[at : at + rows, cols] for w, at in zip(w_refs, places)], axis=0)

    order = list(range(1, heads)) + [0]
    for a, b in zip(order[::2], order[1::2]):
        both = jnp.concatenate([panel(a), panel(b)], axis=1)
        both = jnp.dot(tok[...], both, preferred_element_type=F32)
        out_refs[a][...] = both[:, :HEAD].astype(out_refs[a].dtype)
        out_refs[b][...] = both[:, HEAD:].astype(out_refs[b].dtype)


def product(tok, ws, heads, name):
    total = tok.shape[0]
    return pl.pallas_call(
        functools.partial(product_kernel, heads, [at for _, at in ws]),
        out_shape=[shape(total, HEAD, F32)] + [shape(total, HEAD, BF)] * (heads - 1),
        compiler_params=limit(16),
        name=name,
    )(tok, *[w for w, _ in ws])


def gathered(parts):
    proj = parts[0][...]
    for part in parts[1:]:
        proj = proj + part[...].astype(F32)
    return proj


def score_kernel(heads, *refs):
    parts = refs[:heads]
    query, seg_row, seg_col, key_ref, score_ref = refs[heads:]
    total = query.shape[0]
    count = total // heads
    key = phi(gathered(parts)).astype(BF)
    key_ref[...] = key
    for i in range(heads):
        rows, width = slice(i * count, (i + 1) * count), (i + 1) * count
        scores = lax.dot_general(
            query[rows, :], key[:width, :], (((1,), (1,)), ((), ())), preferred_element_type=F32
        )
        own = jnp.concatenate([seg_col[rows, :]] * (i + 1), axis=1)
        early = lax.broadcasted_iota(jnp.int32, (count, width), 1)
        late = lax.broadcasted_iota(jnp.int32, (count, width), 0) + i * count
        allowed = (own == seg_row[:1, :width]) & (early <= late)
        score_ref[rows, :width] = jnp.where(allowed, scores, 0.0).astype(BF)


def score(parts, query, seg_row, seg_col, heads):
    total = query.shape[0]
    return pl.pallas_call(
        functools.partial(score_kernel, heads),
        out_shape=[shape(total, HEAD, BF), shape(total, total, BF)],
        compiler_params=limit(16),
        cost_estimate=pl.CostEstimate(flops=4 * 10**9, bytes_accessed=0, transcendentals=0),
        name="score",
    )(*parts, query, seg_row, seg_col)


def state_kernel(heads, *refs):
    parts = refs[:heads]
    key, seg_col, state_ref, value_ref = refs[heads:]
    value = gathered(parts).astype(BF)
    last = seg_col[seg_col.shape[0] - 1 :, :]
    tail = jnp.where(seg_col[...] == last, value.astype(F32), 0.0).astype(BF)
    state = lax.dot_general(key[...], tail, (((0,), (0,)), ((), ())), preferred_element_type=F32)
    state_ref[...] = state.astype(state_ref.dtype)
    value_ref[...] = value


def leave(parts, key, seg_col, heads, kind):
    total = seg_col.shape[0]
    return pl.pallas_call(
        functools.partial(state_kernel, heads),
        out_shape=[shape(HEAD, HEAD, kind), shape(total, HEAD, BF)],
        compiler_params=limit(16),
        name="state",
    )(*parts, key, seg_col)


def within_kernel(heads, scores, value, out_ref):
    count = value.shape[0] // heads
    for i in range(heads):
        rows, width = slice(i * count, (i + 1) * count), (i + 1) * count
        out_ref[rows, :] = jnp.dot(scores[rows, :width], value[:width, :], preferred_element_type=F32)


def within(scores, value, heads):
    return pl.pallas_call(
        functools.partial(within_kernel, heads),
        out_shape=shape(value.shape[0], HEAD, F32),
        compiler_params=limit(16),
        cost_estimate=pl.CostEstimate(flops=2 * 10**9, bytes_accessed=0, transcendentals=0),
        name="within",
    )(scores, value)


def finish_kernel(heads, carried, first, inside, gain, *refs):
    out_refs, done = refs[:-1], refs[-1]
    inner, _ = inner_outer(heads)
    count = out_refs[0].shape[0]
    mixed = inside[...] + jnp.dot(first[...], carried[...], preferred_element_type=F32)
    scale = lax.rsqrt(jnp.mean(mixed * mixed, axis=-1, keepdims=True) + 1e-06)
    done[...] = (mixed * scale * gain[:, aligned(inner, HEAD)]).astype(BF)
    for k, out in enumerate(out_refs):
        out[...] = done[aligned(jnp.bitwise_xor(inner, k), count), :]


def finish(carried, first, inside, gain, heads):
    total = first.shape[0]
    return pl.pallas_call(
        functools.partial(finish_kernel, heads),
        out_shape=[shape(total // heads, HEAD, BF)] * heads,
        scratch_shapes=[pltpu.VMEM((total, HEAD), BF)],
        compiler_params=limit(8),
        name="finish",
    )(carried, first, inside, gain)


def join_kernel(heads, *refs):
    inner, _ = inner_outer(heads)
    for k, part in zip(partners(heads), refs[:-1]):
        refs[-1][:, aligned(jnp.bitwise_xor(inner, k), HEAD)] = part[...]


def join(parts, heads):
    return pl.pallas_call(
        functools.partial(join_kernel, heads),
        out_shape=shape(parts[0].shape[0], heads * HEAD, BF),
        compiler_params=limit(8),
        name="join",
    )(*parts)


def on_device(n_ctx, fsdp, tokens, queries, flags, w_key, w_value, norm_gain):
    _, count, depth = tokens.shape
    rows, width = w_key.shape
    heads = width // HEAD
    outer = n_ctx // heads

    def swap(a, mask):
        return lax.ppermute(a, "ctx", [(i, i ^ mask) for i in range(n_ctx)])

    def exchange(parts):
        return [parts[0]] + [swap(parts[k], k) for k in partners(heads)[1:]]

    def other(a):
        return lax.ppermute(a, "fsdp", [(0, 1), (1, 0)])

    both = (w_key, w_value)
    split = outer == 4 and fsdp == 2 and rows == HEAD
    share = fsdp * rows
    if split:
        weights = stack(*both)
        far = swap(weights, 3 * heads)
        packed = pack(tokens[0], queries[0], flags, heads, share)
        weights2, *packed = lax.optimization_barrier((weights, *packed))
        near = swap(weights2, heads)
        received = list(exchange(packed))
        whole = [(w, other(w)) for w in (weights, near, far)]
        away = [far[:rows], far[rows:]]
        last = [swap(away[0], heads)]
        last.append(swap(away[1], heads))
        across = other(last[0])
    else:
        packed = pack(tokens[0], queries[0], flags, heads, share)
        received = exchange(packed)
        groups = [[o * heads + q for o in range(outer)] for q in range(heads)]
        chip = [lax.all_gather(w, "fsdp", axis=0, tiled=True) for w in both]
        full = [lax.all_gather(w, "ctx", axis=0, tiled=True, axis_index_groups=groups) for w in chip]
    tok, query, first, seg_row, seg_col = assemble(received, heads, count, depth // heads, split)
    parts = []
    for i, name in enumerate(("key_product", "value_product")):
        if split:
            if i == 1:
                last[1], parts[0][0] = lax.optimization_barrier((last[1], parts[0][0]))
                across = other(last[1])
            own, close, distant = [[(w, i * rows) for w in pair] for pair in whole]
            panel = own + close + [(last[i], 0), (across, 0)] + distant
        else:
            panel = [(full[i], 0)]
        partial = product(tok, panel, heads, name)
        parts.append(exchange(partial))
    key, scores = score(parts[0], query, seg_row, seg_col, heads)

    doc = DOC_BLOCKS.get(n_ctx, 2 * n_ctx)
    starts = [b for b in range(n_ctx) if b % doc == doc // 2]
    pairs = [
        (b, b + heads)
        for b in range(n_ctx - heads)
        if (b // heads + 1) * heads not in starts
    ]
    rounds = max(1, min(doc // heads, outer) - 1)
    state, value = leave(parts[1], key, seg_col, heads, BF if rounds == 1 else F32)
    carried = lax.ppermute(state.astype(BF), "ctx", pairs)
    keep = (seg_col[-1:, :] == 0.0).astype(F32)
    for _ in range(rounds - 1):
        carried = lax.ppermute((state + keep * carried.astype(F32)).astype(BF), "ctx", pairs)
    inside = within(scores, value, heads)
    done = finish(carried, first, inside, norm_gain.reshape(1, width), heads)
    return join(exchange(done), heads)[None]


def solution(mesh):
    n_ctx, fsdp = mesh.shape["ctx"], mesh.shape["fsdp"]
    in_specs = (
        P("fsdp", "ctx", None),
        P("fsdp", "ctx", None),
        P("fsdp", "ctx"),
        P(("ctx", "fsdp"), None),
        P(("ctx", "fsdp"), None),
        P(),
    )
    return jax.shard_map(
        functools.partial(on_device, n_ctx, fsdp),
        mesh=mesh,
        in_specs=in_specs,
        out_specs=P("fsdp", "ctx", None),
        check_vma=False,
    )
```

```python
import functools

import jax
import jax.numpy as jnp
from jax import lax
from jax.experimental import pallas as pl
from jax.experimental.pallas import tpu as pltpu
from jax.sharding import PartitionSpec as P

HEAD = 128
BF, F32 = jnp.bfloat16, jnp.float32
DOC_BLOCKS = {16: 8, 64: 16}
MARKS = 16
PARTS = 4


def phi(u):
    return jnp.where(u > 0, u + 1.0, jnp.exp(jnp.minimum(u, 0.0)))


def aligned(index, size):
    return pl.ds(pl.multiple_of(index * size, size), size)


def inner_outer(heads):
    me = lax.axis_index("ctx")
    return lax.rem(me, heads), lax.div(me, heads)


def shape(rows, cols, dtype):
    return jax.ShapeDtypeStruct((rows, cols), dtype)


def limit(mib):
    return pltpu.CompilerParams(vmem_limit_bytes=mib * 2**20)


def stack_kernel(*refs):
    parts, out, sems = refs[:-2], refs[-2], refs[-1]
    copies, at = [], 0
    for i, part in enumerate(parts):
        rows = part.shape[0]
        copies.append(pltpu.make_async_copy(part, out.at[at : at + rows, :], sems.at[i]))
        copies[-1].start()
        at += rows
    for copy in copies:
        copy.wait()


def stack(*parts):
    rows = sum(a.shape[0] for a in parts)
    return pl.pallas_call(
        stack_kernel,
        in_specs=[pl.BlockSpec(memory_space=pl.ANY)] * len(parts),
        out_specs=pl.BlockSpec(memory_space=pltpu.VMEM),
        out_shape=pltpu.VMEM((rows, parts[0].shape[1]), BF),
        scratch_shapes=[pltpu.SemaphoreType.DMA((len(parts),))],
        compiler_params=limit(8),
        name="stack",
    )(*[pltpu.with_memory_space_constraint(a, pltpu.HBM) for a in parts])


def partners(heads):
    return [0, heads - 1] + list(range(1, heads - 1))


def pack_kernel(heads, tok_ref, query_ref, flag_ref, *refs):
    out_refs = refs[:heads]
    tok, query, flag, sems = refs[heads:]
    inner, _ = inner_outer(heads)
    count, depth = tok_ref.shape
    squares = depth // (heads * HEAD)
    part = count // PARTS
    pairs = [(query_ref, query), (flag_ref, flag)]
    for p in range(PARTS):
        rows = slice(p * part, (p + 1) * part)
        pairs.append((tok_ref.at[rows, :], tok.at[rows, :]))
    copies = [pltpu.make_async_copy(a, b, sems.at[i]) for i, (a, b) in enumerate(pairs)]
    for copy in copies:
        copy.start()
    for copy in copies[:2]:
        copy.wait()
    marks = jnp.broadcast_to(flag[...].astype(F32), (MARKS, count)).astype(BF)
    for k, out in enumerate(out_refs):
        own = query[:, aligned(jnp.bitwise_xor(inner, k), HEAD)].astype(F32)
        out[squares * count : (squares + 1) * count, :] = phi(own).astype(BF)
        out[(squares + 1) * count :, :] = marks
    for p, copy in enumerate(copies[2:]):
        copy.wait()
        for k, out in enumerate(out_refs):
            to = jnp.bitwise_xor(inner, k)
            for i in range(squares):
                at = ((i // 2) * heads + to) * 2 + i % 2
                rows = slice(i * count + p * part, i * count + (p + 1) * part)
                out[rows, :] = tok[p * part : (p + 1) * part, aligned(at, HEAD)]


def pack(tokens, queries, flags, heads, share):
    count, depth = tokens.shape
    squares = depth // (heads * HEAD)
    if share == 2 * HEAD:
        packed = shape((squares + 1) * count + MARKS, HEAD, BF)
        return pl.pallas_call(
            functools.partial(pack_kernel, heads),
            in_specs=[pl.BlockSpec(memory_space=pl.ANY)] * 3,
            out_specs=[pl.BlockSpec(memory_space=pltpu.VMEM)] * heads,
            out_shape=[pltpu.VMEM(packed.shape, BF)] * heads,
            scratch_shapes=[
                pltpu.VMEM((count, depth), BF),
                pltpu.VMEM((count, heads * HEAD), BF),
                pltpu.VMEM((1, count), jnp.int32),
                pltpu.SemaphoreType.DMA((PARTS + 2,)),
            ],
            compiler_params=limit(8),
            name="pack",
        )(*[pltpu.with_memory_space_constraint(a, pltpu.HBM) for a in (tokens, queries, flags)])
    inner, _ = inner_outer(heads)
    by_inner = tokens.reshape(count, -1, heads, share).transpose(2, 0, 1, 3)
    by_inner = by_inner.reshape(heads, count, squares, HEAD).transpose(0, 2, 1, 3).reshape(heads, -1, HEAD)
    query = phi(queries.astype(F32)).astype(BF).reshape(count, heads, HEAD).transpose(1, 0, 2)
    marks = jnp.broadcast_to(flags.astype(BF), (MARKS, count))
    out = []
    for k in range(heads):
        to = jnp.bitwise_xor(inner, k)
        parts = [lax.dynamic_index_in_dim(a, to, 0, False) for a in (by_inner, query)]
        out.append(jnp.concatenate(parts + [marks], axis=0))
    return out


def assemble_kernel(heads, count, split, *refs):
    x_refs = refs[:heads]
    tok, query, first, seg_row, seg_col, marks = refs[heads:]
    inner, outer = inner_outer(heads)
    squares = tok.shape[1] // HEAD
    total = heads * count
    for k, x in zip(partners(heads), x_refs):
        place = jnp.bitwise_xor(inner, k)
        rows = aligned(place, count)
        for i in range(squares):
            at = i
            if split:
                core = lax.axis_index("fsdp")
                at = jnp.bitwise_xor(outer, i // 2) * 2 + jnp.bitwise_xor(core, i % 2)
            tok[rows, i * HEAD : (i + 1) * HEAD] = x[aligned(at, count), :]
        query[rows, :] = x[squares * count : (squares + 1) * count, :]
        marks[:, rows] = x[(squares + 1) * count :, :]
    early = lax.broadcasted_iota(jnp.int32, (total, total), 0)
    late = lax.broadcasted_iota(jnp.int32, (total, total), 1)
    upto = jnp.where(early <= late, 1.0, 0.0).astype(BF)
    seg = jnp.dot(marks[...], upto, preferred_element_type=F32)[:1, :]
    seg_row[...] = jnp.broadcast_to(seg, seg_row.shape)
    col = jnp.broadcast_to(seg, (HEAD, total)).T
    seg_col[...] = col
    first[...] = jnp.where(col == 0.0, query[...].astype(F32), 0.0).astype(BF)


def assemble(received, heads, count, depth, split):
    total = heads * count
    return pl.pallas_call(
        functools.partial(assemble_kernel, heads, count, split),
        out_shape=[
            shape(total, depth, BF),
            shape(total, HEAD, BF),
            shape(total, HEAD, BF),
            shape(8, total, F32),
            shape(total, HEAD, F32),
        ],
        scratch_shapes=[pltpu.VMEM((MARKS, total), BF)],
        compiler_params=limit(16),
        cost_estimate=pl.CostEstimate(flops=4 * 10**9, bytes_accessed=0, transcendentals=0),
        name="assemble",
    )(*received)


def product_kernel(heads, places, tok, *refs):
    w_refs, out_refs = refs[:-heads], refs[-heads:]
    inner, _ = inner_outer(heads)
    rows = tok.shape[1] // len(places)

    def rows_at(at):
        if at is None:
            return aligned(1 - lax.axis_index("fsdp"), rows)
        return slice(at, at + rows)

    def panel(k):
        cols = aligned(jnp.bitwise_xor(inner, k), HEAD)
        return jnp.concatenate([w[rows_at(at), cols] for w, at in zip(w_refs, places)], axis=0)

    order = list(range(1, heads)) + [0]
    for a, b in zip(order[::2], order[1::2]):
        both = jnp.concatenate([panel(a), panel(b)], axis=1)
        both = jnp.dot(tok[...], both, preferred_element_type=F32)
        out_refs[a][...] = both[:, :HEAD].astype(out_refs[a].dtype)
        out_refs[b][...] = both[:, HEAD:].astype(out_refs[b].dtype)


def product(tok, ws, heads, name):
    total = tok.shape[0]
    return pl.pallas_call(
        functools.partial(product_kernel, heads, [at for _, at in ws]),
        out_shape=[shape(total, HEAD, F32)] + [shape(total, HEAD, BF)] * (heads - 1),
        compiler_params=limit(16),
        name=name,
    )(tok, *[w for w, _ in ws])


def gathered(parts):
    proj = parts[0][...]
    for part in parts[1:]:
        proj = proj + part[...].astype(F32)
    return proj


def score_kernel(heads, *refs):
    parts = refs[:heads]
    query, seg_row, seg_col, key_ref, score_ref = refs[heads:]
    total = query.shape[0]
    count = total // heads
    key = phi(gathered(parts)).astype(BF)
    key_ref[...] = key
    for i in range(heads):
        rows, width = slice(i * count, (i + 1) * count), (i + 1) * count
        scores = lax.dot_general(
            query[rows, :], key[:width, :], (((1,), (1,)), ((), ())), preferred_element_type=F32
        )
        own = jnp.concatenate([seg_col[rows, :]] * (i + 1), axis=1)
        early = lax.broadcasted_iota(jnp.int32, (count, width), 1)
        late = lax.broadcasted_iota(jnp.int32, (count, width), 0) + i * count
        allowed = (own == seg_row[:1, :width]) & (early <= late)
        score_ref[rows, :width] = jnp.where(allowed, scores, 0.0).astype(BF)


def score(parts, query, seg_row, seg_col, heads):
    total = query.shape[0]
    return pl.pallas_call(
        functools.partial(score_kernel, heads),
        out_shape=[shape(total, HEAD, BF), shape(total, total, BF)],
        compiler_params=limit(16),
        cost_estimate=pl.CostEstimate(flops=4 * 10**9, bytes_accessed=0, transcendentals=0),
        name="score",
    )(*parts, query, seg_row, seg_col)


def state_kernel(heads, *refs):
    parts = refs[:heads]
    key, seg_col, state_ref, value_ref = refs[heads:]
    value = gathered(parts).astype(BF)
    last = seg_col[seg_col.shape[0] - 1 :, :]
    tail = jnp.where(seg_col[...] == last, value.astype(F32), 0.0).astype(BF)
    state = lax.dot_general(key[...], tail, (((0,), (0,)), ((), ())), preferred_element_type=F32)
    state_ref[...] = state.astype(state_ref.dtype)
    value_ref[...] = value


def leave(parts, key, seg_col, heads, kind):
    total = seg_col.shape[0]
    return pl.pallas_call(
        functools.partial(state_kernel, heads),
        out_shape=[shape(HEAD, HEAD, kind), shape(total, HEAD, BF)],
        compiler_params=limit(16),
        name="state",
    )(*parts, key, seg_col)


def within_kernel(heads, scores, value, out_ref):
    count = value.shape[0] // heads
    for i in range(heads):
        rows, width = slice(i * count, (i + 1) * count), (i + 1) * count
        out_ref[rows, :] = jnp.dot(scores[rows, :width], value[:width, :], preferred_element_type=F32)


def within(scores, value, heads):
    return pl.pallas_call(
        functools.partial(within_kernel, heads),
        out_shape=shape(value.shape[0], HEAD, F32),
        compiler_params=limit(16),
        cost_estimate=pl.CostEstimate(flops=2 * 10**9, bytes_accessed=0, transcendentals=0),
        name="within",
    )(scores, value)


def finish_kernel(heads, carried, first, inside, gain, *refs):
    out_refs, done = refs[:-1], refs[-1]
    inner, _ = inner_outer(heads)
    count = out_refs[0].shape[0]
    mixed = inside[...] + jnp.dot(first[...], carried[...], preferred_element_type=F32)
    scale = lax.rsqrt(jnp.mean(mixed * mixed, axis=-1, keepdims=True) + 1e-06)
    done[...] = (mixed * scale * gain[:, aligned(inner, HEAD)]).astype(BF)
    for k, out in enumerate(out_refs):
        out[...] = done[aligned(jnp.bitwise_xor(inner, k), count), :]


def finish(carried, first, inside, gain, heads):
    total = first.shape[0]
    return pl.pallas_call(
        functools.partial(finish_kernel, heads),
        out_shape=[shape(total // heads, HEAD, BF)] * heads,
        scratch_shapes=[pltpu.VMEM((total, HEAD), BF)],
        compiler_params=limit(8),
        name="finish",
    )(carried, first, inside, gain)


def join_kernel(heads, *refs):
    inner, _ = inner_outer(heads)
    for k, part in zip(partners(heads), refs[:-1]):
        refs[-1][:, aligned(jnp.bitwise_xor(inner, k), HEAD)] = part[...]


def join(parts, heads):
    return pl.pallas_call(
        functools.partial(join_kernel, heads),
        out_shape=shape(parts[0].shape[0], heads * HEAD, BF),
        compiler_params=limit(8),
        name="join",
    )(*parts)


def on_device(n_ctx, fsdp, tokens, queries, flags, w_key, w_value, norm_gain):
    _, count, depth = tokens.shape
    rows, width = w_key.shape
    heads = width // HEAD
    outer = n_ctx // heads

    def swap(a, mask):
        return lax.ppermute(a, "ctx", [(i, i ^ mask) for i in range(n_ctx)])

    def exchange(parts):
        return [parts[0]] + [swap(parts[k], k) for k in partners(heads)[1:]]

    def other(a):
        return lax.ppermute(a, "fsdp", [(0, 1), (1, 0)])

    both = (w_key, w_value)
    split = outer == 4 and fsdp == 2 and rows == HEAD
    share = fsdp * rows
    if split:
        weights = stack(*both)
        far = swap(weights, 3 * heads)
        packed = pack(tokens[0], queries[0], flags, heads, share)
        held, *packed = lax.optimization_barrier((weights, *packed))
        near = swap(held, heads)
        received = list(exchange(packed))
        whole = [(w, other(w)) for w in (weights, near, far)]
        away = [far[:rows], far[rows:]]
        last = [swap(away[0], heads)]
        last.append(swap(away[1], heads))
        across = other(last[0])
    else:
        packed = pack(tokens[0], queries[0], flags, heads, share)
        received = exchange(packed)
        groups = [[o * heads + q for o in range(outer)] for q in range(heads)]
        chip = [lax.all_gather(w, "fsdp", axis=0, tiled=True) for w in both]
        full = [lax.all_gather(w, "ctx", axis=0, tiled=True, axis_index_groups=groups) for w in chip]
    tok, query, first, seg_row, seg_col = assemble(received, heads, count, depth // heads, split)
    parts = []
    for i, name in enumerate(("key_product", "value_product")):
        if split:
            if i == 1:
                last[1], parts[0][0] = lax.optimization_barrier((last[1], parts[0][0]))
                across = lax.all_gather(last[1], "fsdp", axis=0, tiled=True)
            own, close, distant = [[(w, i * rows) for w in pair] for pair in whole]
            panel = own + close + [(last[i], 0), (across, None if i else 0)] + distant
        else:
            panel = [(full[i], 0)]
        partial = product(tok, panel, heads, name)
        parts.append(exchange(partial))
    key, scores = score(parts[0], query, seg_row, seg_col, heads)

    doc = DOC_BLOCKS.get(n_ctx, 2 * n_ctx)
    starts = [b for b in range(n_ctx) if b % doc == doc // 2]
    pairs = [
        (b, b + heads)
        for b in range(n_ctx - heads)
        if (b // heads + 1) * heads not in starts
    ]
    rounds = max(1, min(doc // heads, outer) - 1)
    state, value = leave(parts[1], key, seg_col, heads, BF if rounds == 1 else F32)
    carried = lax.ppermute(state.astype(BF), "ctx", pairs)
    keep = (seg_col[-1:, :] == 0.0).astype(F32)
    for _ in range(rounds - 1):
        carried = lax.ppermute((state + keep * carried.astype(F32)).astype(BF), "ctx", pairs)
    inside = within(scores, value, heads)
    done = finish(carried, first, inside, norm_gain.reshape(1, width), heads)
    return join(exchange(done), heads)[None]


def solution(mesh):
    n_ctx, fsdp = mesh.shape["ctx"], mesh.shape["fsdp"]
    in_specs = (
        P("fsdp", "ctx", None),
        P("fsdp", "ctx", None),
        P("fsdp", "ctx"),
        P(("ctx", "fsdp"), None),
        P(("ctx", "fsdp"), None),
        P(),
    )
    return jax.shard_map(
        functools.partial(on_device, n_ctx, fsdp),
        mesh=mesh,
        in_specs=in_specs,
        out_specs=P("fsdp", "ctx", None),
        check_vma=False,
    )
```

```python
import functools

import jax
import jax.numpy as jnp
from jax import lax
from jax.experimental import pallas as pl
from jax.experimental.pallas import tpu as pltpu
from jax.sharding import PartitionSpec as P

HEAD = 128
BF, F32 = jnp.bfloat16, jnp.float32
DOC_BLOCKS = {16: 8, 64: 16}
MARKS = 16
PARTS = 4


def phi(u):
    return jnp.where(u > 0, u + 1.0, jnp.exp(jnp.minimum(u, 0.0)))


def aligned(index, size):
    return pl.ds(pl.multiple_of(index * size, size), size)


def inner_outer(heads):
    me = lax.axis_index("ctx")
    return lax.rem(me, heads), lax.div(me, heads)


def shape(rows, cols, dtype):
    return jax.ShapeDtypeStruct((rows, cols), dtype)


def limit(mib):
    return pltpu.CompilerParams(vmem_limit_bytes=mib * 2**20)


def stack_kernel(*refs):
    parts, out, sems = refs[:-2], refs[-2], refs[-1]
    copies, at = [], 0
    for i, part in enumerate(parts):
        rows = part.shape[0]
        copies.append(pltpu.make_async_copy(part, out.at[at : at + rows, :], sems.at[i]))
        copies[-1].start()
        at += rows
    for copy in copies:
        copy.wait()


def stack(*parts):
    rows = sum(a.shape[0] for a in parts)
    return pl.pallas_call(
        stack_kernel,
        in_specs=[pl.BlockSpec(memory_space=pl.ANY)] * len(parts),
        out_specs=pl.BlockSpec(memory_space=pltpu.VMEM),
        out_shape=pltpu.VMEM((rows, parts[0].shape[1]), BF),
        scratch_shapes=[pltpu.SemaphoreType.DMA((len(parts),))],
        compiler_params=limit(8),
        name="stack",
    )(*[pltpu.with_memory_space_constraint(a, pltpu.HBM) for a in parts])


def partners(heads):
    return [0, heads - 1] + list(range(1, heads - 1))


def token_partners(heads):
    return partners(heads)


def pack_kernel(heads, tok_ref, query_ref, flag_ref, *refs):
    out_refs = refs[:heads]
    tok, query, flag, sems = refs[heads:]
    inner, _ = inner_outer(heads)
    count, depth = tok_ref.shape
    squares = depth // (heads * HEAD)
    part = count // PARTS
    pairs = [(query_ref, query), (flag_ref, flag)]
    for p in range(PARTS):
        rows = slice(p * part, (p + 1) * part)
        pairs.append((tok_ref.at[rows, :], tok.at[rows, :]))
    copies = [pltpu.make_async_copy(a, b, sems.at[i]) for i, (a, b) in enumerate(pairs)]
    for copy in copies:
        copy.start()
    for copy in copies[:2]:
        copy.wait()
    marks = jnp.broadcast_to(flag[...].astype(F32), (MARKS, count)).astype(BF)
    for k, out in enumerate(out_refs):
        own = query[:, aligned(jnp.bitwise_xor(inner, k), HEAD)].astype(F32)
        out[squares * count : (squares + 1) * count, :] = phi(own).astype(BF)
        out[(squares + 1) * count :, :] = marks
    for p, copy in enumerate(copies[2:]):
        copy.wait()
        for k, out in enumerate(out_refs):
            to = jnp.bitwise_xor(inner, k)
            for i in range(squares):
                at = ((i // 2) * heads + to) * 2 + i % 2
                rows = slice(i * count + p * part, i * count + (p + 1) * part)
                out[rows, :] = tok[p * part : (p + 1) * part, aligned(at, HEAD)]


def pack(tokens, queries, flags, heads, share):
    count, depth = tokens.shape
    squares = depth // (heads * HEAD)
    if share == 2 * HEAD:
        packed = shape((squares + 1) * count + MARKS, HEAD, BF)
        return pl.pallas_call(
            functools.partial(pack_kernel, heads),
            in_specs=[pl.BlockSpec(memory_space=pl.ANY)] * 3,
            out_specs=[pl.BlockSpec(memory_space=pltpu.VMEM)] * heads,
            out_shape=[pltpu.VMEM(packed.shape, BF)] * heads,
            scratch_shapes=[
                pltpu.VMEM((count, depth), BF),
                pltpu.VMEM((count, heads * HEAD), BF),
                pltpu.VMEM((1, count), jnp.int32),
                pltpu.SemaphoreType.DMA((PARTS + 2,)),
            ],
            compiler_params=limit(8),
            name="pack",
        )(*[pltpu.with_memory_space_constraint(a, pltpu.HBM) for a in (tokens, queries, flags)])
    inner, _ = inner_outer(heads)
    by_inner = tokens.reshape(count, -1, heads, share).transpose(2, 0, 1, 3)
    by_inner = by_inner.reshape(heads, count, squares, HEAD).transpose(0, 2, 1, 3).reshape(heads, -1, HEAD)
    query = phi(queries.astype(F32)).astype(BF).reshape(count, heads, HEAD).transpose(1, 0, 2)
    marks = jnp.broadcast_to(flags.astype(BF), (MARKS, count))
    out = []
    for k in range(heads):
        to = jnp.bitwise_xor(inner, k)
        parts = [lax.dynamic_index_in_dim(a, to, 0, False) for a in (by_inner, query)]
        out.append(jnp.concatenate(parts + [marks], axis=0))
    return out


def assemble_kernel(heads, count, split, *refs):
    x_refs = refs[:heads]
    tok, query, first, seg_row, seg_col, marks = refs[heads:]
    inner, outer = inner_outer(heads)
    squares = tok.shape[1] // HEAD
    total = heads * count
    for k, x in zip(token_partners(heads), x_refs):
        place = jnp.bitwise_xor(inner, k)
        rows = aligned(place, count)
        for i in range(squares):
            at = i
            if split:
                core = lax.axis_index("fsdp")
                at = jnp.bitwise_xor(outer, i // 2) * 2 + jnp.bitwise_xor(core, i % 2)
            tok[rows, i * HEAD : (i + 1) * HEAD] = x[aligned(at, count), :]
        query[rows, :] = x[squares * count : (squares + 1) * count, :]
        marks[:, rows] = x[(squares + 1) * count :, :]
    early = lax.broadcasted_iota(jnp.int32, (total, total), 0)
    late = lax.broadcasted_iota(jnp.int32, (total, total), 1)
    upto = jnp.where(early <= late, 1.0, 0.0).astype(BF)
    seg = jnp.dot(marks[...], upto, preferred_element_type=F32)[:1, :]
    seg_row[...] = jnp.broadcast_to(seg, seg_row.shape)
    col = jnp.broadcast_to(seg, (HEAD, total)).T
    seg_col[...] = col
    first[...] = jnp.where(col == 0.0, query[...].astype(F32), 0.0).astype(BF)


def assemble(received, heads, count, depth, split):
    total = heads * count
    return pl.pallas_call(
        functools.partial(assemble_kernel, heads, count, split),
        out_shape=[
            shape(total, depth, BF),
            shape(total, HEAD, BF),
            shape(total, HEAD, BF),
            shape(8, total, F32),
            shape(total, HEAD, F32),
        ],
        scratch_shapes=[pltpu.VMEM((MARKS, total), BF)],
        compiler_params=limit(16),
        cost_estimate=pl.CostEstimate(flops=4 * 10**9, bytes_accessed=0, transcendentals=0),
        name="assemble",
    )(*received)


def product_kernel(heads, places, tok, *refs):
    w_refs, out_refs = refs[:-heads], refs[-heads:]
    inner, _ = inner_outer(heads)
    rows = tok.shape[1] // len(places)

    def rows_at(at):
        if isinstance(at, tuple):
            other = 1 - lax.axis_index("fsdp")
            return pl.ds(pl.multiple_of(other * at[0] + at[1], rows), rows)
        return slice(at, at + rows)

    def panel(k):
        cols = aligned(jnp.bitwise_xor(inner, k), HEAD)
        return jnp.concatenate([w[rows_at(at), cols] for w, at in zip(w_refs, places)], axis=0)

    order = list(range(1, heads)) + [0]
    for a, b in zip(order[::2], order[1::2]):
        both = jnp.concatenate([panel(a), panel(b)], axis=1)
        both = jnp.dot(tok[...], both, preferred_element_type=F32)
        out_refs[a][...] = both[:, :HEAD].astype(out_refs[a].dtype)
        out_refs[b][...] = both[:, HEAD:].astype(out_refs[b].dtype)


def product(tok, ws, heads, name):
    total = tok.shape[0]
    return pl.pallas_call(
        functools.partial(product_kernel, heads, [at for _, at in ws]),
        out_shape=[shape(total, HEAD, F32)] + [shape(total, HEAD, BF)] * (heads - 1),
        compiler_params=limit(16),
        name=name,
    )(tok, *[w for w, _ in ws])


def gathered(parts):
    proj = parts[0][...]
    for part in parts[1:]:
        proj = proj + part[...].astype(F32)
    return proj


def score_kernel(heads, *refs):
    parts = refs[:heads]
    query, seg_row, seg_col, key_ref, score_ref = refs[heads:]
    total = query.shape[0]
    count = total // heads
    key = phi(gathered(parts)).astype(BF)
    key_ref[...] = key
    for i in range(heads):
        rows, width = slice(i * count, (i + 1) * count), (i + 1) * count
        scores = lax.dot_general(
            query[rows, :], key[:width, :], (((1,), (1,)), ((), ())), preferred_element_type=F32
        )
        own = jnp.concatenate([seg_col[rows, :]] * (i + 1), axis=1)
        early = lax.broadcasted_iota(jnp.int32, (count, width), 1)
        late = lax.broadcasted_iota(jnp.int32, (count, width), 0) + i * count
        allowed = (own == seg_row[:1, :width]) & (early <= late)
        score_ref[rows, :width] = jnp.where(allowed, scores, 0.0).astype(BF)


def score(parts, query, seg_row, seg_col, heads):
    total = query.shape[0]
    return pl.pallas_call(
        functools.partial(score_kernel, heads),
        out_shape=[shape(total, HEAD, BF), shape(total, total, BF)],
        compiler_params=limit(16),
        cost_estimate=pl.CostEstimate(flops=4 * 10**9, bytes_accessed=0, transcendentals=0),
        name="score",
    )(*parts, query, seg_row, seg_col)


def state_kernel(heads, *refs):
    parts = refs[:heads]
    key, seg_col, state_ref, value_ref = refs[heads:]
    value = gathered(parts).astype(BF)
    last = seg_col[seg_col.shape[0] - 1 :, :]
    tail = jnp.where(seg_col[...] == last, value.astype(F32), 0.0).astype(BF)
    state = lax.dot_general(key[...], tail, (((0,), (0,)), ((), ())), preferred_element_type=F32)
    state_ref[...] = state.astype(state_ref.dtype)
    value_ref[...] = value


def leave(parts, key, seg_col, heads, kind):
    total = seg_col.shape[0]
    return pl.pallas_call(
        functools.partial(state_kernel, heads),
        out_shape=[shape(HEAD, HEAD, kind), shape(total, HEAD, BF)],
        compiler_params=limit(16),
        name="state",
    )(*parts, key, seg_col)


def within_kernel(heads, scores, value, out_ref):
    count = value.shape[0] // heads
    for i in range(heads):
        rows, width = slice(i * count, (i + 1) * count), (i + 1) * count
        out_ref[rows, :] = jnp.dot(scores[rows, :width], value[:width, :], preferred_element_type=F32)


def within(scores, value, heads):
    return pl.pallas_call(
        functools.partial(within_kernel, heads),
        out_shape=shape(value.shape[0], HEAD, F32),
        compiler_params=limit(16),
        cost_estimate=pl.CostEstimate(flops=2 * 10**9, bytes_accessed=0, transcendentals=0),
        name="within",
    )(scores, value)


def finish_kernel(heads, carried, first, inside, gain, *refs):
    out_refs, done = refs[:-1], refs[-1]
    inner, _ = inner_outer(heads)
    count = out_refs[0].shape[0]
    mixed = inside[...] + jnp.dot(first[...], carried[...], preferred_element_type=F32)
    scale = lax.rsqrt(jnp.mean(mixed * mixed, axis=-1, keepdims=True) + 1e-06)
    done[...] = (mixed * scale * gain[:, aligned(inner, HEAD)]).astype(BF)
    for k, out in enumerate(out_refs):
        out[...] = done[aligned(jnp.bitwise_xor(inner, k), count), :]


def finish(carried, first, inside, gain, heads):
    total = first.shape[0]
    return pl.pallas_call(
        functools.partial(finish_kernel, heads),
        out_shape=[shape(total // heads, HEAD, BF)] * heads,
        scratch_shapes=[pltpu.VMEM((total, HEAD), BF)],
        compiler_params=limit(8),
        name="finish",
    )(carried, first, inside, gain)


def join_kernel(heads, *refs):
    inner, _ = inner_outer(heads)
    for k, part in zip(partners(heads), refs[:-1]):
        refs[-1][:, aligned(jnp.bitwise_xor(inner, k), HEAD)] = part[...]


def join(parts, heads):
    return pl.pallas_call(
        functools.partial(join_kernel, heads),
        out_shape=shape(parts[0].shape[0], heads * HEAD, BF),
        compiler_params=limit(8),
        name="join",
    )(*parts)


def on_device(n_ctx, fsdp, tokens, queries, flags, w_key, w_value, norm_gain):
    _, count, depth = tokens.shape
    rows, width = w_key.shape
    heads = width // HEAD
    outer = n_ctx // heads

    def swap(a, mask):
        return lax.ppermute(a, "ctx", [(i, i ^ mask) for i in range(n_ctx)])

    def exchange(parts, order=partners):
        return [parts[0]] + [swap(parts[k], k) for k in order(heads)[1:]]

    def other(a):
        return lax.ppermute(a, "fsdp", [(0, 1), (1, 0)])

    both = (w_key, w_value)
    split = outer == 4 and fsdp == 2 and rows == HEAD
    share = fsdp * rows
    if split:
        weights = stack(*both)
        far = swap(weights, 3 * heads)
        packed = pack(tokens[0], queries[0], flags, heads, share)
        held, *packed = lax.optimization_barrier((weights, *packed))
        near = swap(held, heads)
        received = exchange(packed, token_partners)
        mine = lax.all_gather(weights, "fsdp", axis=0, tiled=True)
        mine, far = lax.optimization_barrier((mine, far))
        whole = [(w, other(w)) for w in (near, far)]
        away = [far[:rows], far[rows:]]
        last = [swap(away[0], heads)]
        last.append(swap(away[1], heads))
        across = other(last[0])
    else:
        packed = pack(tokens[0], queries[0], flags, heads, share)
        received = exchange(packed, token_partners)
        groups = [[o * heads + q for o in range(outer)] for q in range(heads)]
        chip = [lax.all_gather(w, "fsdp", axis=0, tiled=True) for w in both]
        full = [lax.all_gather(w, "ctx", axis=0, tiled=True, axis_index_groups=groups) for w in chip]
    tok, query, first, seg_row, seg_col = assemble(received, heads, count, depth // heads, split)
    parts = []
    for i, name in enumerate(("key_product", "value_product")):
        if split:
            if i == 1:
                last[1], parts[0][0] = lax.optimization_barrier((last[1], parts[0][0]))
                across = lax.all_gather(last[1], "fsdp", axis=0, tiled=True)
            close, distant = [[(w, i * rows) for w in pair] for pair in whole]
            own = [(weights, i * rows), (mine, (2 * rows, i * rows))]
            panel = own + close + [(last[i], 0), (across, (rows, 0) if i else 0)] + distant
        else:
            panel = [(full[i], 0)]
        partial = product(tok, panel, heads, name)
        parts.append(exchange(partial))
    key, scores = score(parts[0], query, seg_row, seg_col, heads)

    doc = DOC_BLOCKS.get(n_ctx, 2 * n_ctx)
    starts = [b for b in range(n_ctx) if b % doc == doc // 2]
    pairs = [
        (b, b + heads)
        for b in range(n_ctx - heads)
        if (b // heads + 1) * heads not in starts
    ]
    rounds = max(1, min(doc // heads, outer) - 1)
    state, value = leave(parts[1], key, seg_col, heads, BF if rounds == 1 else F32)
    carried = lax.ppermute(state.astype(BF), "ctx", pairs)
    keep = (seg_col[-1:, :] == 0.0).astype(F32)
    for _ in range(rounds - 1):
        carried = lax.ppermute((state + keep * carried.astype(F32)).astype(BF), "ctx", pairs)
    inside = within(scores, value, heads)
    done = finish(carried, first, inside, norm_gain.reshape(1, width), heads)
    return join(exchange(done), heads)[None]


def solution(mesh):
    n_ctx, fsdp = mesh.shape["ctx"], mesh.shape["fsdp"]
    in_specs = (
        P("fsdp", "ctx", None),
        P("fsdp", "ctx", None),
        P("fsdp", "ctx"),
        P(("ctx", "fsdp"), None),
        P(("ctx", "fsdp"), None),
        P(),
    )
    return jax.shard_map(
        functools.partial(on_device, n_ctx, fsdp),
        mesh=mesh,
        in_specs=in_specs,
        out_specs=P("fsdp", "ctx", None),
        check_vma=False,
    )
```
